256 devices in a mesh: segment: 4 (over x_lo, core), lat: 16 (over z, x_hi), lon: 4 (over y).
Axes of the slice: x: 4 (x_hi: 2, x_lo: 2; x = x_hi * 2 + x_lo), y: 4, z: 8, core: 2. Of those that a mesh axis runs over, the one named last changes fastest.
Arguments:
- fields: bfloat16 [4, 192, 24, 512], P(None, 'lat', 'lon'), may hold values from -6 to 6
- cotangent: bfloat16 [4, 192, 24, 512], P(None, 'lat', 'lon'), may hold values from -6 to 6
- depths: int32 [4], P('segment'), may hold values from 1 to 2, as said below
- w_qkv: bfloat16 [4, 2, 512, 1536], P('segment'), may hold values from -0.25 to 0.25
- w_out: bfloat16 [4, 2, 512, 512], P('segment'), may hold values from -0.25 to 0.25
Outputs:
- segment_out: bfloat16 [4, 4, 192, 24, 512], P('segment', None, 'lat', 'lon')
- segment_grad: float32 [4, 4, 192, 24, 512], P('segment', None, 'lat', 'lon')
- qkv_grad: float32 [4, 2, 512, 1536], P('segment', None, ('lat', 'lon'))
- out_grad: float32 [4, 2, 512, 512], P('segment', None, ('lat', 'lon'))
The draws below stay inside these ranges and needn't reach their ends.
Inputs may be any that keep to these rules, and one draw needn't show every extreme that they name: Each section runs its first depths layers; some section runs all 2 layers and some only one.
All inputs are finite; a program needn't handle non-finite values.
Results may differ from the reference program's by a relative error of at most 0.028.
Values may be sent and summed in bfloat16 or wider, within the bound.
A program may use at most 192 MiB of HBM per device.

```python
import jax
import jax.numpy as jnp
from jax import lax

D = 512
HEADS = 8
HS = 64
WIN_LEV = 2
WIN_LAT = 12
WIN_LON = 6
MAXL = 2
SEGMENTS = 4
LEV = 4
LAT = 192
LON = 24


def draw_depths(key, part):
    key = jax.random.fold_in(key, 11)
    key_base, key_order = jax.random.split(key)
    base = jax.random.randint(key_base, (SEGMENTS,), 1, MAXL + 1)
    order = jax.random.permutation(key_order, SEGMENTS)
    base = base.at[order[0]].set(MAXL)
    base = base.at[order[1]].set(1)
    return base.astype(jnp.int32)


def block_scale(key, extent, pieces, smallest, largest):
    level = 1.0
    for dim, parts in pieces:
        heights = jax.random.uniform(jax.random.fold_in(jax.random.fold_in(key, 6), dim), (parts,), jnp.float32, smallest / len(pieces), largest / len(pieces))
        level = level * jnp.repeat(jnp.exp(heights), extent[dim] // parts).reshape((-1,) + (1,) * (len(extent) - 1 - dim))
    return level


def normal_values(rng, shape, deviation, limit, shards=(), dtype=jnp.bfloat16):
    entries = jax.random.normal(rng, shape, jnp.float32) * deviation
    if len(shards) > 0:
        entries = block_scale(rng, shape, shards, -0.22, 0.18) * entries
    return jnp.clip(entries, min=-limit, max=limit).astype(dtype)


def setup_inputs(seed: int = 0) -> dict:
    arg_keys = jax.random.split(jax.random.key(seed), 6)
    return {
        "fields": normal_values(arg_keys[0], (LEV, LAT, LON, D), 1.0, 6.0, ((1, 16), (2, 4))),
        "cotangent": normal_values(arg_keys[1], (LEV, LAT, LON, D), 1.0, 6.0, ((1, 16), (2, 4))),
        "depths": draw_depths(jax.random.fold_in(arg_keys[5], 71), 0),
        "w_qkv": normal_values(arg_keys[3], (SEGMENTS, MAXL, D, 3 * D), D ** -0.5, 0.25, ((0, 4),)),
        "w_out": normal_values(arg_keys[4], (SEGMENTS, MAXL, D, D), D ** -0.5, 0.25, ((0, 4),)),
    }


EPSILON = 1e-05

def normalize(stream):
    center = stream - lax.optimization_barrier(jnp.mean(stream, axis=-1, keepdims=True))
    inverse = lax.rsqrt(lax.optimization_barrier(jnp.mean(center * center, axis=-1, keepdims=True)) + EPSILON)
    return (center * inverse, inverse)

def norm_back(scaled, inverse, gradient):
    middle = gradient - lax.optimization_barrier(jnp.mean(gradient, axis=-1, keepdims=True))
    return inverse * (middle - scaled * lax.optimization_barrier(jnp.mean(gradient * scaled, axis=-1, keepdims=True)))

def project(inputs, weight):
    flattened = inputs.reshape(-1, inputs.shape[-1])
    result = jnp.dot(flattened, weight, preferred_element_type=jnp.float32)
    return result.reshape(inputs.shape[:-1] + (weight.shape[-1],))

def transpose_dot(left_rows, right_rows):
    return jnp.dot(left_rows.reshape(-1, left_rows.shape[-1]).T, right_rows.reshape(-1, right_rows.shape[-1]), preferred_element_type=jnp.float32)

def to_windows(field, height):
    level_count, band_rows, strip_cols, channels = field.shape
    shaped = field.reshape(level_count // WIN_LEV, WIN_LEV, band_rows // height, height, strip_cols // WIN_LON, WIN_LON, channels)
    shaped = shaped.transpose(0, 2, 4, 1, 3, 5, 6)
    return shaped.reshape(-1, WIN_LEV * height * WIN_LON, channels)

def from_windows(windows, level_count, band_rows, strip_cols, height):
    channels = windows.shape[-1]
    shaped = windows.reshape(level_count // WIN_LEV, band_rows // height, strip_cols // WIN_LON, WIN_LEV, height, WIN_LON, channels)
    shaped = shaped.transpose(0, 3, 1, 4, 2, 5, 6)
    return shaped.reshape(level_count, band_rows, strip_cols, channels)

def attend(queries, key_rows, key_valid, w_qkv, w_out):
    model_width = queries.shape[-1]
    queried = project(queries, w_qkv[:, :model_width]).astype(jnp.bfloat16)
    keyvals = project(key_rows, w_qkv[:, model_width:]).astype(jnp.bfloat16)
    qheads = queried.reshape(queried.shape[:2] + (HEADS, HS))
    kheads = keyvals[..., :model_width].reshape(keyvals.shape[:2] + (HEADS, HS))
    vheads = keyvals[..., model_width:].reshape(keyvals.shape[:2] + (HEADS, HS))
    score_scale = HS ** (-0.5)
    scores = jnp.einsum('bqhe,bkhe->bhqk', qheads.astype(jnp.float32), kheads.astype(jnp.float32)) * score_scale
    exponent = jnp.exp(scores) * key_valid[:, None, None, :]
    attn_probs = exponent / lax.optimization_barrier(jnp.sum(exponent, axis=-1, keepdims=True))
    probs_low = attn_probs.astype(jnp.bfloat16)
    mixed = jnp.einsum('bhqk,bkhe->bqhe', probs_low.astype(jnp.float32), vheads.astype(jnp.float32))
    mixed_low = mixed.reshape(queried.shape).astype(jnp.bfloat16)
    branch = project(mixed_low, w_out)
    return (branch, (qheads, kheads, vheads, attn_probs, probs_low, mixed_low))

def attend_back(gradient, stored, w_out):
    qheads, kheads, vheads, attn_probs, probs_low, mixed_low = stored
    model_width = w_out.shape[0]
    score_scale = HS ** (-0.5)
    grad_low = gradient.astype(jnp.bfloat16)
    grad_out = transpose_dot(mixed_low, grad_low)
    grad_mixed = project(grad_low, w_out.T).astype(jnp.bfloat16).reshape(qheads.shape)
    grad_probs = jnp.einsum('bqhe,bkhe->bhqk', grad_mixed.astype(jnp.float32), vheads.astype(jnp.float32))
    grad_values = jnp.einsum('bhqk,bqhe->bkhe', probs_low.astype(jnp.float32), grad_mixed.astype(jnp.float32))
    inner = lax.optimization_barrier(jnp.sum(attn_probs * grad_probs, axis=-1, keepdims=True))
    grad_scores = (attn_probs * (grad_probs - inner) * score_scale).astype(jnp.bfloat16)
    grad_query = jnp.einsum('bhqk,bkhe->bqhe', grad_scores.astype(jnp.float32), kheads.astype(jnp.float32))
    grad_keys = jnp.einsum('bhqk,bqhe->bkhe', grad_scores.astype(jnp.float32), qheads.astype(jnp.float32))
    grad_query = grad_query.reshape(grad_query.shape[:2] + (model_width,))
    grad_pairs = jnp.concatenate([grad_keys.reshape(grad_keys.shape[:2] + (model_width,)), grad_values.reshape(grad_values.shape[:2] + (model_width,))], axis=-1)
    return (grad_out, grad_query, grad_pairs)

def finish(queries, key_rows, grad_query, grad_pairs, w_qkv):
    model_width = queries.shape[-1]
    query_low = grad_query.astype(jnp.bfloat16)
    pairs_low = grad_pairs.astype(jnp.bfloat16)
    grad_weight = jnp.concatenate([transpose_dot(queries, query_low), transpose_dot(key_rows, pairs_low)], axis=1)
    part_query = project(query_low, w_qkv[:, :model_width].T)
    part_keys = project(pairs_low, w_qkv[:, model_width:].T)
    return (grad_weight, part_query, part_keys)

def segment_forward(stream, depth_here, w_qkv, w_out):
    level_count, band_rows, strip_cols, model_width = stream.shape
    half_rows = WIN_LAT // 2
    pads = ((0, 0), (half_rows, half_rows), (0, 0), (0, 0))
    kept_state = []
    for sublayer in range(MAXL):
        scaled, inverse = normalize(stream)
        normed = scaled.astype(jnp.bfloat16)
        if sublayer % 2 == 0:
            key_rows = to_windows(normed, WIN_LAT)
            key_valid = jnp.ones(key_rows.shape[:2], jnp.float32)
            branch, stored = attend(key_rows, key_rows, key_valid, w_qkv[sublayer], w_out[sublayer])
            branch = from_windows(branch, level_count, band_rows, strip_cols, WIN_LAT)
        else:
            key_rows = to_windows(jnp.pad(normed, pads), WIN_LAT)
            mask_field = jnp.pad(jnp.ones((level_count, band_rows, strip_cols, 1), jnp.float32), pads)
            key_valid = to_windows(mask_field, WIN_LAT)[..., 0]
            branch, stored = attend(key_rows, key_rows, key_valid, w_qkv[sublayer], w_out[sublayer])
            branch = from_windows(branch, level_count, band_rows + 2 * half_rows, strip_cols, WIN_LAT)[:, half_rows:half_rows + band_rows]
        active = (sublayer < depth_here).astype(jnp.float32)
        stream = stream + active * branch
        kept_state.append((scaled, inverse, key_rows, stored, active))
    return (stream, kept_state)

def segment_backward(gradient, kept_state, w_qkv, w_out):
    level_count, band_rows, strip_cols, model_width = gradient.shape
    half_rows = WIN_LAT // 2
    pads = ((0, 0), (half_rows, half_rows), (0, 0), (0, 0))
    qkv_terms = [None] * MAXL
    out_terms = [None] * MAXL
    for sublayer in reversed(range(MAXL)):
        scaled, inverse, key_rows, stored, active = kept_state[sublayer]
        branch_grad = gradient * active
        if sublayer % 2 == 0:
            windowed = to_windows(branch_grad, WIN_LAT)
        else:
            windowed = to_windows(jnp.pad(branch_grad, pads), WIN_LAT)
        grad_out, grad_query, grad_pairs = attend_back(windowed, stored, w_out[sublayer])
        grad_weight, part_query, part_keys = finish(key_rows, key_rows, grad_query, grad_pairs, w_qkv[sublayer])
        grad_normed = part_query + part_keys
        if sublayer % 2 == 0:
            grad_normed = from_windows(grad_normed, level_count, band_rows, strip_cols, WIN_LAT)
        else:
            grad_normed = from_windows(grad_normed, level_count, band_rows + 2 * half_rows, strip_cols, WIN_LAT)[:, half_rows:half_rows + band_rows]
        gradient = gradient + norm_back(scaled, inverse, grad_normed)
        qkv_terms[sublayer] = grad_weight
        out_terms[sublayer] = grad_out
    return (gradient, jnp.stack(qkv_terms), jnp.stack(out_terms))

def reference(fields, cotangent, depths, w_qkv, w_out):
    outputs = []
    kept_all = []
    for segment_no in range(SEGMENTS):
        if segment_no == 0:
            stream = fields.astype(jnp.float32)
        elif segment_no == SEGMENTS - 1:
            stream = outputs[-1].astype(jnp.float32) + outputs[0].astype(jnp.float32)
        else:
            stream = outputs[-1].astype(jnp.float32)
        result, kept_state = segment_forward(stream, depths[segment_no], w_qkv[segment_no], w_out[segment_no])
        outputs.append(result.astype(jnp.bfloat16))
        kept_all.append(kept_state)
    input_grads = [None] * SEGMENTS
    qkv_grads = [None] * SEGMENTS
    out_grads = [None] * SEGMENTS
    for segment_no in reversed(range(SEGMENTS)):
        if segment_no == SEGMENTS - 1:
            gradient = cotangent.astype(jnp.float32)
        elif segment_no == 0:
            gradient = input_grads[1] + input_grads[SEGMENTS - 1]
        else:
            gradient = input_grads[segment_no + 1]
        input_grads[segment_no], qkv_grads[segment_no], out_grads[segment_no] = segment_backward(gradient, kept_all[segment_no], w_qkv[segment_no], w_out[segment_no])
    return (jnp.stack(outputs), jnp.stack(input_grads), jnp.stack(qkv_grads), jnp.stack(out_grads))
```

```python
from functools import partial

import jax
import jax.numpy as jnp
from jax import lax
from jax.experimental import pallas as pl
from jax.experimental.pallas import tpu as pltpu
from jax.sharding import PartitionSpec as P

HEADS = 8
HS = 64
WIN_LEV = 2
WIN_LON = 6
MAXL = 2
D = 512
PAIRS = 4
HALF = 72
TOK = 144
EPSILON = 1e-05
MESH = pl.DeviceIdType.MESH
F32 = jnp.float32
BF16 = jnp.bfloat16


def dot(a, b, contract):
    return lax.dot_general(a, b, ((contract[:1], contract[1:]), ((), ())), preferred_element_type=F32)


def normalize(stream):
    center = stream - jnp.mean(stream, axis=-1, keepdims=True)
    inverse = lax.rsqrt(jnp.mean(center * center, axis=-1, keepdims=True) + EPSILON)
    return (center * inverse, inverse)


def norm_back(scaled, inverse, gradient):
    middle = gradient - jnp.mean(gradient, axis=-1, keepdims=True)
    return inverse * (middle - scaled * jnp.mean(gradient * scaled, axis=-1, keepdims=True))


def split_heads(value):
    low = lax.broadcasted_iota(jnp.int32, value.shape, 1) < HS
    return jnp.concatenate([jnp.where(low, value, 0.0), jnp.where(low, 0.0, value)], axis=0).astype(BF16)


def join_heads(value):
    count = value.shape[0] // 2
    low = lax.broadcasted_iota(jnp.int32, (count, value.shape[1]), 1) < HS
    return jnp.where(low, value[:count], value[count:])


def window_forward(q2, k, v, valid):
    exponent = jnp.exp(dot(q2, k, (1, 1)) * (HS ** -0.5))
    if valid is not None:
        exponent = exponent * valid
    probs = exponent * (1.0 / jnp.sum(exponent, axis=-1, keepdims=True))
    return probs, join_heads(dot(probs.astype(BF16), v, (1, 0)))


def window_backward(gm2, q2, k, v, probs):
    grad_probs = dot(gm2, v, (1, 1))
    inner = jnp.sum(probs * grad_probs, axis=-1, keepdims=True)
    grad_scores = (probs * (grad_probs - inner) * (HS ** -0.5)).astype(BF16)
    gq = join_heads(dot(grad_scores, k, (1, 0)))
    gk = dot(grad_scores, q2, (0, 0))
    gv = dot(probs.astype(BF16), gm2, (0, 0))
    return gq, gk, gv


def body(
    lat_total,
    fields_ref, cot_ref, active_ref, wqkv_hbm, wout_hbm,
    out_ref, grad_ref, term_ref,
    wqkv_s, wout_s, act_s, xin, gin, stream_s, g_s, outs, out_in, grads, grad_in, handoff,
    nrm, halo, rim, rim_in, xs, invs, probs_s, q2_s, kv_s, left, left_in, right, right_in,
    own_sem, w_send, w_recv, a_sem, x_send, x_recv, g_send, g_recv, o_send, o_recv, s_send, s_recv,
    h_send, h_recv, r_send, r_recv, l_send, l_recv, t_send, t_recv,
):
    seg = lax.axis_index("segment")
    lat = lax.axis_index("lat")
    lon = lax.axis_index("lon")
    core = lax.rem(seg, 2)
    first = seg < 2
    has_prev = lat > 0
    has_next = lat < lat_total - 1
    partner = {"segment": seg + 1 - 2 * core, "lat": lat, "lon": lon}
    across = {"segment": lax.rem(seg + 2, 4), "lat": lat, "lon": lon}
    prev = {"segment": seg, "lat": lax.rem(lat + lat_total - 1, lat_total), "lon": lon}
    nxt = {"segment": seg, "lat": lax.rem(lat + 1, lat_total), "lon": lon}

    def remote(src, dst, send, recv, to):
        return pltpu.make_async_remote_copy(
            src_ref=src, dst_ref=dst, send_sem=send, recv_sem=recv, device_id=to, device_id_type=MESH
        )

    barrier = pltpu.get_barrier_semaphore()
    pl.semaphore_signal(barrier, inc=1, device_id=partner, device_id_type=MESH)
    pl.semaphore_signal(barrier, inc=1, device_id=across, device_id_type=MESH)

    @pl.when(has_prev)
    def _():
        pl.semaphore_signal(barrier, inc=1, device_id=prev, device_id_type=MESH)

    @pl.when(has_next)
    def _():
        pl.semaphore_signal(barrier, inc=1, device_id=nxt, device_id_type=MESH)

    def own_w(layer):
        return (
            pltpu.make_async_copy(wqkv_hbm.at[layer], wqkv_s.at[core, layer], own_sem.at[layer, 0]),
            pltpu.make_async_copy(wout_hbm.at[layer], wout_s.at[core, layer], own_sem.at[layer, 1]),
        )

    def sent_w(layer):
        return (
            remote(wqkv_hbm.at[layer], wqkv_s.at[core, layer], w_send.at[layer, 0], w_recv.at[layer, 0], partner),
            remote(wout_hbm.at[layer], wout_s.at[core, layer], w_send.at[layer, 1], w_recv.at[layer, 1], partner),
        )

    def came_w(layer):
        other = 1 - core
        return (
            remote(wqkv_hbm.at[layer], wqkv_s.at[other, layer], w_send.at[layer, 0], w_recv.at[layer, 0], partner),
            remote(wout_hbm.at[layer], wout_s.at[other, layer], w_send.at[layer, 1], w_recv.at[layer, 1], partner),
        )

    for layer in range(MAXL):
        for copy in own_w(layer):
            copy.start()

    act_s[core] = active_ref[...]

    @pl.when(first)
    def _():
        xin[0] = fields_ref[...]
        xin[1] = jnp.zeros((TOK, D), BF16)

    @pl.when(jnp.logical_not(first))
    def _():
        gin[0] = cot_ref[...]
        gin[1] = jnp.zeros((TOK, D), BF16)

    @pl.when(jnp.logical_not(has_prev))
    def _():
        halo[0, 0] = jnp.zeros((HALF, D), BF16)
        halo[1, 0] = jnp.zeros((HALF, D), BF16)
        rim_in[0, 0] = jnp.zeros((HALF, 2 * D), BF16)
        rim_in[1, 0] = jnp.zeros((HALF, 2 * D), BF16)

    @pl.when(jnp.logical_not(has_next))
    def _():
        halo[0, 1] = jnp.zeros((HALF, D), BF16)
        halo[1, 1] = jnp.zeros((HALF, D), BF16)
        rim_in[0, 1] = jnp.zeros((HALF, 2 * D), BF16)
        rim_in[1, 1] = jnp.zeros((HALF, 2 * D), BF16)

    pl.semaphore_wait(barrier, 2 + has_prev.astype(jnp.int32) + has_next.astype(jnp.int32))

    sent_act = remote(active_ref, act_s.at[core], a_sem.at[0], a_sem.at[1], partner)
    came_act = remote(active_ref, act_s.at[1 - core], a_sem.at[0], a_sem.at[1], partner)
    sent_act.start()
    for layer in range(MAXL):
        for copy in sent_w(layer):
            copy.start()

    def halo_prev(sl):
        return remote(nrm.at[sl, 0], halo.at[sl, 1], h_send.at[sl, 0], h_recv.at[sl, 1], prev)

    def halo_next(sl):
        return remote(nrm.at[sl, 1], halo.at[sl, 0], h_send.at[sl, 1], h_recv.at[sl, 0], nxt)

    def rim_prev(sl):
        return remote(rim.at[sl, 0], rim_in.at[sl, 1], r_send.at[sl, 0], r_recv.at[sl, 1], prev)

    def rim_next(sl):
        return remote(rim.at[sl, 1], rim_in.at[sl, 0], r_send.at[sl, 1], r_recv.at[sl, 0], nxt)

    def start_pair(to_prev, to_next):
        @pl.when(has_prev)
        def _():
            to_prev.start()

        @pl.when(has_next)
        def _():
            to_next.start()

    def arrive_pair(to_prev, to_next):
        @pl.when(has_prev)
        def _():
            to_next.wait_recv()

        @pl.when(has_next)
        def _():
            to_prev.wait_recv()

    def left_pair(to_prev, to_next):
        @pl.when(has_prev)
        def _():
            to_prev.wait_send()

        @pl.when(has_next)
        def _():
            to_next.wait_send()

    def rows_left(sl, layer):
        return remote(left.at[sl, layer], left_in.at[layer], l_send.at[layer], l_recv.at[layer], partner)

    def rows_right(sl, layer):
        return remote(right.at[sl, layer], right_in.at[layer], t_send.at[layer], t_recv.at[layer], partner)

    act_copy = remote(outs.at[1], xin.at[0], x_send.at[0], x_recv.at[0], across)
    skip_copy = remote(outs.at[0], xin.at[1], x_send.at[1], x_recv.at[1], across)
    gact_copy = remote(handoff.at[0], gin.at[0], g_send.at[0], g_recv.at[0], across)
    gskip_copy = remote(handoff.at[1], gin.at[1], g_send.at[1], g_recv.at[1], across)

    def out_copy(sl):
        return remote(outs.at[sl], out_in, o_send, o_recv, partner)

    def grad_copy(sl):
        return remote(grads.at[sl], grad_in, s_send, s_recv, partner)

    prev_valid = has_prev.astype(F32)
    next_valid = has_next.astype(F32)
    key_at = lax.broadcasted_iota(jnp.int32, (1, TOK), 1)
    valid_a = jnp.where(key_at < HALF, prev_valid, 1.0)
    valid_b = jnp.where(key_at < HALF, 1.0, next_valid)

    def weights_ready(sl, layer):
        @pl.when(core == sl)
        def _():
            for copy in own_w(layer):
                copy.wait()

        @pl.when(core != sl)
        def _():
            for copy in came_w(layer):
                copy.wait_recv()

    @pl.when(jnp.logical_not(first))
    def _():
        act_copy.wait_recv()

    stream_s[...] = xin[0].astype(F32)

    def forward(sl, carry):
        stream = stream_s[...]
        scaled, inverse = normalize(stream)
        normed = scaled.astype(BF16)
        xs[sl, 0] = scaled
        invs[sl, 0] = jnp.broadcast_to(inverse, (TOK, 128))
        left[sl, 0, :, :D] = normed
        weights_ready(sl, 0)
        qkv = dot(normed, wqkv_s[sl, 0], (1, 0))
        kv_low = qkv[:, D:].astype(BF16)
        kv_s[sl, 0] = kv_low
        mixed = []
        for p in range(PAIRS):
            at = slice(128 * p, 128 * p + 128)
            q2 = split_heads(qkv[:, at])
            q2_s[sl, 0, p] = q2
            probs, mix = window_forward(q2, kv_low[:, at], kv_low[:, D + 128 * p : D + 128 * p + 128], None)
            probs_s[sl, 0, p] = probs
            mixed.append(mix)
        mixed_low = jnp.concatenate(mixed, axis=1).astype(BF16)
        left[sl, 0, :, D:] = mixed_low
        stream = stream + dot(mixed_low, wout_s[sl, 0], (1, 0))

        scaled, inverse = normalize(stream)
        normed = scaled.astype(BF16)
        nrm[sl, 0] = scaled[:HALF].astype(BF16)
        nrm[sl, 1] = scaled[HALF:].astype(BF16)
        to_prev, to_next = halo_prev(sl), halo_next(sl)
        start_pair(to_prev, to_next)
        xs[sl, 1] = scaled
        invs[sl, 1] = jnp.broadcast_to(inverse, (TOK, 128))
        left[sl, 1, :, :D] = normed
        weights_ready(sl, 1)

        @pl.when(core != sl)
        def _():
            rows_left(sl, 0).start()

        qkv = dot(normed, wqkv_s[sl, 1], (1, 0))
        arrive_pair(to_prev, to_next)
        beside = jnp.concatenate([halo[sl, 0].astype(F32), halo[sl, 1].astype(F32)], axis=0).astype(BF16)
        kv_beside = dot(beside, wqkv_s[sl, 1, :, D:], (1, 0))
        kv_a = jnp.concatenate([kv_beside[:HALF], qkv[:HALF, D:]], axis=0).astype(BF16)
        kv_b = jnp.concatenate([qkv[HALF:, D:], kv_beside[HALF:]], axis=0).astype(BF16)
        kv_s[sl, 1] = kv_a
        kv_s[sl, 2] = kv_b
        mixed = []
        for p in range(PAIRS):
            at = slice(128 * p, 128 * p + 128)
            vat = slice(D + 128 * p, D + 128 * p + 128)
            qa = split_heads(qkv[:HALF, at])
            qb = split_heads(qkv[HALF:, at])
            q2_s[sl, 1, p, :TOK] = qa
            q2_s[sl, 1, p, TOK:] = qb
            probs_a, mix_a = window_forward(qa, kv_a[:, at], kv_a[:, vat], valid_a)
            probs_b, mix_b = window_forward(qb, kv_b[:, at], kv_b[:, vat], valid_b)
            probs_s[sl, 1, p, :TOK] = probs_a
            probs_s[sl, 1, p, TOK:] = probs_b
            mixed.append(jnp.concatenate([mix_a, mix_b], axis=0))
        mixed_low = jnp.concatenate(mixed, axis=1).astype(BF16)
        left[sl, 1, :, D:] = mixed_low

        @pl.when(core != sl)
        def _():
            came_act.wait_recv()
            rows_left(sl, 1).start()

        stream = stream + act_s[sl][0:1, 0:1] * dot(mixed_low, wout_s[sl, 1], (1, 0))
        low = stream.astype(BF16)
        outs[sl] = low

        @pl.when(core != sl)
        def _():
            out_copy(sl).start()

        @pl.when(sl == 0)
        def _():
            @pl.when(first)
            def _():
                skip_copy.start()

            @pl.when(jnp.logical_not(first))
            def _():
                skip_copy.wait_recv()

            stream_s[...] = low.astype(F32) + xin[1].astype(F32)

        return carry

    lax.fori_loop(0, 2, forward, 0)

    @pl.when(first)
    def _():
        act_copy.start()
        gact_copy.wait_recv()

    g_s[...] = gin[0].astype(F32)

    def backward(step, carry):
        sl = 1 - step
        g = g_s[...]
        glow = (g * act_s[sl][0:1, 0:1]).astype(BF16)
        right[sl, 1, :, 3 * D :] = glow
        gm = dot(glow, wout_s[sl, 1], (1, 1))
        gq, gka, gva, gkb, gvb = [], [], [], [], []
        for p in range(PAIRS):
            at = slice(128 * p, 128 * p + 128)
            vat = slice(D + 128 * p, D + 128 * p + 128)
            qa, ka, va = window_backward(
                split_heads(gm[:HALF, at]), q2_s[sl, 1, p, :TOK], kv_s[sl, 1, :, at], kv_s[sl, 1, :, vat],
                probs_s[sl, 1, p, :TOK],
            )
            qb, kb, vb = window_backward(
                split_heads(gm[HALF:, at]), q2_s[sl, 1, p, TOK:], kv_s[sl, 2, :, at], kv_s[sl, 2, :, vat],
                probs_s[sl, 1, p, TOK:],
            )
            gq.append(jnp.concatenate([qa, qb], axis=0))
            gka.append(ka)
            gva.append(va)
            gkb.append(kb)
            gvb.append(vb)
        pair_a = jnp.concatenate(gka + gva, axis=1)
        pair_b = jnp.concatenate(gkb + gvb, axis=1)
        rim[sl, 0] = pair_a[:HALF].astype(BF16)
        rim[sl, 1] = pair_b[HALF:].astype(BF16)
        to_prev, to_next = rim_prev(sl), rim_next(sl)
        start_pair(to_prev, to_next)
        query_low = jnp.concatenate(gq, axis=1).astype(BF16)
        right[sl, 1, :, :D] = query_low
        part = dot(query_low, wqkv_s[sl, 1, :, :D], (1, 1))
        arrive_pair(to_prev, to_next)
        pairs_low = jnp.concatenate(
            [pair_a[HALF:] + rim_in[sl, 0].astype(F32), pair_b[:HALF] + rim_in[sl, 1].astype(F32)], axis=0
        ).astype(BF16)
        right[sl, 1, :, D : 3 * D] = pairs_low

        @pl.when(core != sl)
        def _():
            rows_right(sl, 1).start()

        part = part + dot(pairs_low, wqkv_s[sl, 1, :, D:], (1, 1))
        g = g + norm_back(xs[sl, 1], invs[sl, 1][:, 0:1], part)

        glow = g.astype(BF16)
        right[sl, 0, :, 3 * D :] = glow
        gm = dot(glow, wout_s[sl, 0], (1, 1))
        gq, gk, gv = [], [], []
        for p in range(PAIRS):
            at = slice(128 * p, 128 * p + 128)
            vat = slice(D + 128 * p, D + 128 * p + 128)
            q, k, v = window_backward(
                split_heads(gm[:, at]), q2_s[sl, 0, p], kv_s[sl, 0, :, at], kv_s[sl, 0, :, vat], probs_s[sl, 0, p]
            )
            gq.append(q)
            gk.append(k)
            gv.append(v)
        low = jnp.concatenate(gq + gk + gv, axis=1).astype(BF16)
        right[sl, 0, :, : 3 * D] = low

        @pl.when(core != sl)
        def _():
            rows_right(sl, 0).start()

        part = dot(low, wqkv_s[sl, 0], (1, 1))
        g = g + norm_back(xs[sl, 0], invs[sl, 0][:, 0:1], part)
        grads[sl] = g

        @pl.when(core != sl)
        def _():
            grad_copy(sl).start()

        @pl.when(jnp.logical_not(first))
        def _():
            handoff[1 - step] = g.astype(BF16)

            @pl.when(step == 0)
            def _():
                gskip_copy.start()

            @pl.when(step == 1)
            def _():
                gact_copy.start()

        @pl.when(step == 0)
        def _():
            @pl.when(first)
            def _():
                gskip_copy.wait_recv()

            g_s[...] = g + gin[1].astype(F32)

        return carry

    lax.fori_loop(0, 2, backward, 0)

    def weight_terms(layer, carry):
        rows_left(core, layer).wait_recv()
        rows_right(core, layer).wait_recv()
        for tile in range(4):
            lhs_at = slice(0, D) if tile < 3 else slice(D, 2 * D)
            rhs_at = slice(D * tile, D * tile + D)
            lhs = jnp.concatenate([left[core, layer, :, lhs_at], left_in[layer, :, lhs_at]], axis=0)
            rhs = jnp.concatenate([right[core, layer, :, rhs_at], right_in[layer, :, rhs_at]], axis=0)
            term_ref[layer, tile] = dot(lhs, rhs, (0, 0)).astype(term_ref.dtype)
        return carry

    lax.fori_loop(0, MAXL, weight_terms, 0)

    out_copy(core).wait_recv()
    grad_copy(core).wait_recv()
    out_ref[core] = outs[core]
    out_ref[1 - core] = out_in[...]
    grad_ref[core] = grads[core]
    grad_ref[1 - core] = grad_in[...]

    sent_act.wait_send()

    for layer in range(MAXL):
        for copy in sent_w(layer):
            copy.wait_send()
        rows_left(1 - core, layer).wait_send()
        rows_right(1 - core, layer).wait_send()
    out_copy(1 - core).wait_send()
    grad_copy(1 - core).wait_send()
    for sl in range(2):
        left_pair(halo_prev(sl), halo_next(sl))
        left_pair(rim_prev(sl), rim_next(sl))

    @pl.when(first)
    def _():
        act_copy.wait_send()
        skip_copy.wait_send()

    @pl.when(jnp.logical_not(first))
    def _():
        gact_copy.wait_send()
        gskip_copy.wait_send()


def network(fields, cotangent, active, w_qkv, w_out, lat_total):
    vmem = pl.BlockSpec(memory_space=pltpu.VMEM)
    hbm = pl.BlockSpec(memory_space=pl.ANY)
    dma = pltpu.SemaphoreType.DMA
    scratch = [
        pltpu.VMEM((2, MAXL, D, 3 * D), BF16),
        pltpu.VMEM((2, MAXL, D, D), BF16),
        pltpu.VMEM((2, 8, 128), F32),
        pltpu.VMEM((2, TOK, D), BF16),
        pltpu.VMEM((2, TOK, D), BF16),
        pltpu.VMEM((TOK, D), F32),
        pltpu.VMEM((TOK, D), F32),
        pltpu.VMEM((2, TOK, D), BF16),
        pltpu.VMEM((TOK, D), BF16),
        pltpu.VMEM((2, TOK, D), F32),
        pltpu.VMEM((TOK, D), F32),
        pltpu.VMEM((2, TOK, D), BF16),
        pltpu.VMEM((2, 2, HALF, D), BF16),
        pltpu.VMEM((2, 2, HALF, D), BF16),
        pltpu.VMEM((2, 2, HALF, 2 * D), BF16),
        pltpu.VMEM((2, 2, HALF, 2 * D), BF16),
        pltpu.VMEM((2, MAXL, TOK, D), F32),
        pltpu.VMEM((2, MAXL, TOK, 128), F32),
        pltpu.VMEM((2, MAXL, PAIRS, 2 * TOK, TOK), F32),
        pltpu.VMEM((2, MAXL, PAIRS, 2 * TOK, 128), BF16),
        pltpu.VMEM((2, 3, TOK, 2 * D), BF16),
        pltpu.VMEM((2, MAXL, TOK, 2 * D), BF16),
        pltpu.VMEM((MAXL, TOK, 2 * D), BF16),
        pltpu.VMEM((2, MAXL, TOK, 4 * D), BF16),
        pltpu.VMEM((MAXL, TOK, 4 * D), BF16),
        dma((MAXL, 2)),
        dma((MAXL, 2)),
        dma((MAXL, 2)),
        dma((2,)),
        dma((2,)),
        dma((2,)),
        dma((2,)),
        dma((2,)),
        dma,
        dma,
        dma,
        dma,
        dma((2, 2)),
        dma((2, 2)),
        dma((2, 2)),
        dma((2, 2)),
        dma((MAXL,)),
        dma((MAXL,)),
        dma((MAXL,)),
        dma((MAXL,)),
    ]
    return pl.pallas_call(
        partial(body, lat_total),
        out_shape=(
            jax.ShapeDtypeStruct((2, TOK, D), BF16),
            jax.ShapeDtypeStruct((2, TOK, D), F32),
            jax.ShapeDtypeStruct((MAXL, 4, D, D), BF16),
        ),
        in_specs=[vmem, vmem, vmem, hbm, hbm],
        out_specs=(vmem, vmem, vmem),
        scratch_shapes=scratch,
        compiler_params=pltpu.CompilerParams(
            collective_id=0, has_side_effects=True, vmem_limit_bytes=56 * 1024 * 1024
        ),
        name="network",
    )(fields, cotangent, active, w_qkv, w_out)


def to_rows(cells, core):
    pair = lax.dynamic_slice_in_dim(cells, 2 * core, 2, axis=0)
    return pair.reshape(WIN_LEV, 2, 6, WIN_LON, D).transpose(1, 0, 2, 3, 4).reshape(TOK, D)


def from_rows(rows):
    shaped = rows.reshape(2, 2, WIN_LEV, 6, WIN_LON, D).transpose(0, 2, 1, 3, 4, 5)
    return shaped.reshape(1, 2 * WIN_LEV, 12, WIN_LON, D)


def local(fields, cotangent, depths, w_qkv, w_out):
    core = lax.rem(lax.axis_index("segment"), 2)
    active = jnp.broadcast_to((depths[0] > 1).astype(F32), (8, 128))
    out_rows, grad_rows, terms = network(
        to_rows(fields, core), to_rows(cotangent, core), active, w_qkv[0], w_out[0], lax.axis_size("lat")
    )
    lats, lons = lax.axis_size("lat"), lax.axis_size("lon")
    pieces = terms.reshape(MAXL, 4, lats, lons, D // (lats * lons), D)
    part = lax.all_to_all(pieces, "lon", 3, 3, tiled=True).astype(F32).sum(3).astype(BF16)
    summed = lax.all_to_all(part, "lat", 2, 2, tiled=True).astype(F32).sum(2)
    shaped = summed.transpose(0, 2, 1, 3).reshape(MAXL, -1, 4 * D)
    return (
        from_rows(out_rows),
        from_rows(grad_rows),
        shaped[None, :, :, : 3 * D],
        shaped[None, :, :, 3 * D :],
    )


def solution(mesh):
    placed = (
        P(None, "lat", "lon", None),
        P(None, "lat", "lon", None),
        P("segment"),
        P("segment", None, None, None),
        P("segment", None, None, None),
    )
    return jax.shard_map(
        local,
        mesh=mesh,
        in_specs=placed,
        out_specs=(
            P("segment", None, "lat", "lon", None),
            P("segment", None, "lat", "lon", None),
            P("segment", None, ("lat", "lon"), None),
            P("segment", None, ("lat", "lon"), None),
        ),
        check_vma=False,
    )
```

```python
from functools import partial

import jax
import jax.numpy as jnp
from jax import lax
from jax.experimental import pallas as pl
from jax.experimental.pallas import tpu as pltpu
from jax.sharding import PartitionSpec as P

HEADS = 8
HS = 64
WIN_LEV = 2
WIN_LON = 6
MAXL = 2
D = 512
PAIRS = 4
HALF = 72
TOK = 144
EPSILON = 1e-05
MESH = pl.DeviceIdType.MESH
F32 = jnp.float32
BF16 = jnp.bfloat16


def dot(a, b, contract):
    return lax.dot_general(a, b, ((contract[:1], contract[1:]), ((), ())), preferred_element_type=F32)


def normalize(stream):
    center = stream - jnp.mean(stream, axis=-1, keepdims=True)
    inverse = lax.rsqrt(jnp.mean(center * center, axis=-1, keepdims=True) + EPSILON)
    return (center * inverse, inverse)


def norm_back(scaled, inverse, gradient):
    middle = gradient - jnp.mean(gradient, axis=-1, keepdims=True)
    return inverse * (middle - scaled * jnp.mean(gradient * scaled, axis=-1, keepdims=True))


def split_heads(value):
    low = lax.broadcasted_iota(jnp.int32, value.shape, 1) < HS
    return jnp.concatenate([jnp.where(low, value, 0.0), jnp.where(low, 0.0, value)], axis=0).astype(BF16)


def join_heads(value):
    count = value.shape[0] // 2
    low = lax.broadcasted_iota(jnp.int32, (count, value.shape[1]), 1) < HS
    return jnp.where(low, value[:count], value[count:])


def window_forward(q2, k, v, valid):
    exponent = jnp.exp(dot(q2, k, (1, 1)) * (HS ** -0.5))
    if valid is not None:
        exponent = exponent * valid
    probs = exponent * (1.0 / jnp.sum(exponent, axis=-1, keepdims=True))
    return probs, join_heads(dot(probs.astype(BF16), v, (1, 0)))


def window_backward(gm2, q2, k, v, probs):
    grad_probs = dot(gm2, v, (1, 1))
    inner = jnp.sum(probs * grad_probs, axis=-1, keepdims=True)
    grad_scores = (probs * (grad_probs - inner) * (HS ** -0.5)).astype(BF16)
    gq = join_heads(dot(grad_scores, k, (1, 0)))
    gk = dot(grad_scores, q2, (0, 0))
    gv = dot(probs.astype(BF16), gm2, (0, 0))
    return gq, gk, gv


def body(
    lat_total, lon_total,
    fields_ref, cot_ref, active_ref, wqkv_hbm, wout_hbm,
    out_ref, grad_ref, term_ref,
    wqkv_s, wout_s, act_s, xin, gin, stream_s, g_s, outs, out_in, grads, grad_in, handoff,
    nrm, halo, rim, rim_in, xs, invs, probs_s, q2_s, kv_s, left, left_in, right, right_in,
    part_s, part_in, mid_s, mid_in, fin_s, fin_in,
    own_sem, w_send, w_recv, a_sem, x_send, x_recv, g_send, g_recv, o_send, o_recv, s_send, s_recv,
    h_send, h_recv, r_send, r_recv, l_send, l_recv, t_send, t_recv,
    y_send, y_recv, z_send, z_recv, f_send, f_recv,
):
    seg = lax.axis_index("segment")
    lat = lax.axis_index("lat")
    lon = lax.axis_index("lon")
    core = lax.rem(seg, 2)
    first = seg < 2
    has_prev = lat > 0
    has_next = lat < lat_total - 1
    partner = {"segment": seg + 1 - 2 * core, "lat": lat, "lon": lon}
    across = {"segment": lax.rem(seg + 2, 4), "lat": lat, "lon": lon}
    prev = {"segment": seg, "lat": lax.rem(lat + lat_total - 1, lat_total), "lon": lon}
    nxt = {"segment": seg, "lat": lax.rem(lat + 1, lat_total), "lon": lon}

    def remote(src, dst, send, recv, to):
        return pltpu.make_async_remote_copy(
            src_ref=src, dst_ref=dst, send_sem=send, recv_sem=recv, device_id=to, device_id_type=MESH
        )

    barrier = pltpu.get_barrier_semaphore()
    pl.semaphore_signal(barrier, inc=1, device_id=partner, device_id_type=MESH)
    pl.semaphore_signal(barrier, inc=1, device_id=across, device_id_type=MESH)

    def lon_peer(hop):
        return {"segment": seg, "lat": lat, "lon": lax.rem(lon + hop, lon_total)}

    def lat_peer(hop):
        return {"segment": seg, "lat": lax.rem(lat + hop, lat_total), "lon": lon}

    def greet_lon(hop, carry):
        pl.semaphore_signal(barrier, inc=1, device_id=lon_peer(hop), device_id_type=MESH)
        return carry

    def greet_lat(hop, carry):
        pl.semaphore_signal(barrier, inc=1, device_id=lat_peer(hop), device_id_type=MESH)
        return carry

    lax.fori_loop(1, lon_total, greet_lon, 0)
    lax.fori_loop(1, lat_total, greet_lat, 0)

    def own_w(layer):
        return (
            pltpu.make_async_copy(wqkv_hbm.at[layer], wqkv_s.at[core, layer], own_sem.at[layer, 0]),
            pltpu.make_async_copy(wout_hbm.at[layer], wout_s.at[core, layer], own_sem.at[layer, 1]),
        )

    def sent_w(layer):
        return (
            remote(wqkv_hbm.at[layer], wqkv_s.at[core, layer], w_send.at[layer, 0], w_recv.at[layer, 0], partner),
            remote(wout_hbm.at[layer], wout_s.at[core, layer], w_send.at[layer, 1], w_recv.at[layer, 1], partner),
        )

    def came_w(layer):
        other = 1 - core
        return (
            remote(wqkv_hbm.at[layer], wqkv_s.at[other, layer], w_send.at[layer, 0], w_recv.at[layer, 0], partner),
            remote(wout_hbm.at[layer], wout_s.at[other, layer], w_send.at[layer, 1], w_recv.at[layer, 1], partner),
        )

    for layer in range(MAXL):
        for copy in own_w(layer):
            copy.start()

    act_s[core] = active_ref[...]

    @pl.when(first)
    def _():
        xin[0] = fields_ref[...]
        xin[1] = jnp.zeros((TOK, D), BF16)

    @pl.when(jnp.logical_not(first))
    def _():
        gin[0] = cot_ref[...]
        gin[1] = jnp.zeros((TOK, D), BF16)

    @pl.when(jnp.logical_not(has_prev))
    def _():
        halo[0, 0] = jnp.zeros((HALF, D), BF16)
        halo[1, 0] = jnp.zeros((HALF, D), BF16)
        rim_in[0, 0] = jnp.zeros((HALF, 2 * D), BF16)
        rim_in[1, 0] = jnp.zeros((HALF, 2 * D), BF16)

    @pl.when(jnp.logical_not(has_next))
    def _():
        halo[0, 1] = jnp.zeros((HALF, D), BF16)
        halo[1, 1] = jnp.zeros((HALF, D), BF16)
        rim_in[0, 1] = jnp.zeros((HALF, 2 * D), BF16)
        rim_in[1, 1] = jnp.zeros((HALF, 2 * D), BF16)

    pl.semaphore_wait(barrier, lon_total + lat_total)

    sent_act = remote(active_ref, act_s.at[core], a_sem.at[0], a_sem.at[1], partner)
    came_act = remote(active_ref, act_s.at[1 - core], a_sem.at[0], a_sem.at[1], partner)
    sent_act.start()
    for layer in range(MAXL):
        for copy in sent_w(layer):
            copy.start()

    def halo_prev(sl):
        return remote(nrm.at[sl, 0], halo.at[sl, 1], h_send.at[sl, 0], h_recv.at[sl, 1], prev)

    def halo_next(sl):
        return remote(nrm.at[sl, 1], halo.at[sl, 0], h_send.at[sl, 1], h_recv.at[sl, 0], nxt)

    def rim_prev(sl):
        return remote(rim.at[sl, 0], rim_in.at[sl, 1], r_send.at[sl, 0], r_recv.at[sl, 1], prev)

    def rim_next(sl):
        return remote(rim.at[sl, 1], rim_in.at[sl, 0], r_send.at[sl, 1], r_recv.at[sl, 0], nxt)

    def start_pair(to_prev, to_next):
        @pl.when(has_prev)
        def _():
            to_prev.start()

        @pl.when(has_next)
        def _():
            to_next.start()

    def arrive_pair(to_prev, to_next):
        @pl.when(has_prev)
        def _():
            to_next.wait_recv()

        @pl.when(has_next)
        def _():
            to_prev.wait_recv()

    def left_pair(to_prev, to_next):
        @pl.when(has_prev)
        def _():
            to_prev.wait_send()

        @pl.when(has_next)
        def _():
            to_next.wait_send()

    def rows_left(unit):
        return remote(left.at[unit], left_in.at[unit], l_send.at[unit], l_recv.at[unit], partner)

    def rows_right(unit):
        return remote(right.at[unit, 1 - core], right_in.at[unit], t_send.at[unit], t_recv.at[unit], partner)

    def part_copy(unit, hop):
        to = lax.rem(lon + hop, lon_total)
        return remote(
            part_s.at[unit, to], part_in.at[unit, hop - 1], y_send.at[unit, hop - 1], y_recv.at[unit, hop - 1], lon_peer(hop)
        )

    def mid_copy(unit, hop):
        to = lax.rem(lat + hop, lat_total)
        return remote(
            mid_s.at[unit, to], mid_in.at[unit, hop - 1], z_send.at[unit, hop - 1], z_recv.at[unit, hop - 1], lat_peer(hop)
        )

    def fin_copy(layer):
        return remote(fin_s.at[1 - core, layer], fin_in.at[layer], f_send.at[layer], f_recv.at[layer], partner)

    def weight_term(unit):
        rows_left(unit).wait_recv()
        rows_right(unit).wait_recv()
        normed = jnp.concatenate([left[unit, 0], left_in[unit, 0]], axis=0)
        second = jnp.concatenate([left[unit, core], left_in[unit, core]], axis=0)
        grads_low = jnp.concatenate([right[unit, core], right_in[unit]], axis=0)
        group = lat_total * lon_total
        one = dot(normed, grads_low[:, :D], (0, 0)).reshape(lat_total, lon_total, D // group, D)
        two = dot(second, grads_low[:, D:], (0, 0)).reshape(lat_total, lon_total, D // group, D)
        both = jnp.concatenate([one, two], axis=2).astype(BF16)
        for to in range(lon_total):
            part_s[unit, to] = both[:, to]
        for hop in range(1, lon_total):
            part_copy(unit, hop).start()

    def middle(unit, carry):
        total = part_s[unit, lon].astype(F32)
        for hop in range(1, lon_total):
            part_copy(unit, hop).wait_recv()
            total = total + part_in[unit, hop - 1].astype(F32)
        mid_s[unit] = total.astype(BF16)

        def send(hop, inner):
            mid_copy(unit, hop).start()
            return inner

        return lax.fori_loop(1, lat_total, send, carry)

    def last(unit):
        def add(hop, total):
            mid_copy(unit, hop).wait_recv()
            return total + mid_in[unit, hop - 1].astype(F32)

        return lax.fori_loop(1, lat_total, add, mid_s[unit, lat].astype(F32))

    act_copy = remote(outs.at[1], xin.at[0], x_send.at[0], x_recv.at[0], across)
    skip_copy = remote(outs.at[0], xin.at[1], x_send.at[1], x_recv.at[1], across)
    gact_copy = remote(handoff.at[0], gin.at[0], g_send.at[0], g_recv.at[0], across)
    gskip_copy = remote(handoff.at[1], gin.at[1], g_send.at[1], g_recv.at[1], across)

    def out_copy(sl):
        return remote(outs.at[sl], out_in, o_send, o_recv, partner)

    def grad_copy(sl):
        return remote(grads.at[sl], grad_in, s_send, s_recv, partner)

    prev_valid = has_prev.astype(F32)
    next_valid = has_next.astype(F32)
    key_at = lax.broadcasted_iota(jnp.int32, (1, TOK), 1)
    valid_a = jnp.where(key_at < HALF, prev_valid, 1.0)
    valid_b = jnp.where(key_at < HALF, 1.0, next_valid)

    def weights_ready(sl, layer):
        @pl.when(core == sl)
        def _():
            for copy in own_w(layer):
                copy.wait()

        @pl.when(core != sl)
        def _():
            for copy in came_w(layer):
                copy.wait_recv()

    @pl.when(jnp.logical_not(first))
    def _():
        act_copy.wait_recv()

    stream_s[...] = xin[0].astype(F32)

    def forward(sl, carry):
        stream = stream_s[...]
        scaled, inverse = normalize(stream)
        normed = scaled.astype(BF16)
        xs[sl, 0] = scaled
        invs[sl, 0] = jnp.broadcast_to(inverse, (TOK, 128))
        left[2 * sl, 0] = normed
        weights_ready(sl, 0)
        qkv = dot(normed, wqkv_s[sl, 0], (1, 0))
        kv_low = qkv[:, D:].astype(BF16)
        kv_s[sl, 0] = kv_low
        mixed = []
        for p in range(PAIRS):
            at = slice(128 * p, 128 * p + 128)
            q2 = split_heads(qkv[:, at])
            q2_s[sl, 0, p] = q2
            probs, mix = window_forward(q2, kv_low[:, at], kv_low[:, D + 128 * p : D + 128 * p + 128], None)
            probs_s[sl, 0, p] = probs
            mixed.append(mix)
        mixed_low = jnp.concatenate(mixed, axis=1).astype(BF16)
        left[2 * sl, 1] = mixed_low
        stream = stream + dot(mixed_low, wout_s[sl, 0], (1, 0))

        scaled, inverse = normalize(stream)
        normed = scaled.astype(BF16)
        nrm[sl, 0] = scaled[:HALF].astype(BF16)
        nrm[sl, 1] = scaled[HALF:].astype(BF16)
        to_prev, to_next = halo_prev(sl), halo_next(sl)
        start_pair(to_prev, to_next)
        xs[sl, 1] = scaled
        invs[sl, 1] = jnp.broadcast_to(inverse, (TOK, 128))
        left[2 * sl + 1, 0] = normed
        weights_ready(sl, 1)

        rows_left(2 * sl).start()
        qkv = dot(normed, wqkv_s[sl, 1], (1, 0))
        arrive_pair(to_prev, to_next)
        beside = jnp.concatenate([halo[sl, 0].astype(F32), halo[sl, 1].astype(F32)], axis=0).astype(BF16)
        kv_beside = dot(beside, wqkv_s[sl, 1, :, D:], (1, 0))
        kv_a = jnp.concatenate([kv_beside[:HALF], qkv[:HALF, D:]], axis=0).astype(BF16)
        kv_b = jnp.concatenate([qkv[HALF:, D:], kv_beside[HALF:]], axis=0).astype(BF16)
        kv_s[sl, 1] = kv_a
        kv_s[sl, 2] = kv_b
        mixed = []
        for p in range(PAIRS):
            at = slice(128 * p, 128 * p + 128)
            vat = slice(D + 128 * p, D + 128 * p + 128)
            qa = split_heads(qkv[:HALF, at])
            qb = split_heads(qkv[HALF:, at])
            q2_s[sl, 1, p, :TOK] = qa
            q2_s[sl, 1, p, TOK:] = qb
            probs_a, mix_a = window_forward(qa, kv_a[:, at], kv_a[:, vat], valid_a)
            probs_b, mix_b = window_forward(qb, kv_b[:, at], kv_b[:, vat], valid_b)
            probs_s[sl, 1, p, :TOK] = probs_a
            probs_s[sl, 1, p, TOK:] = probs_b
            mixed.append(jnp.concatenate([mix_a, mix_b], axis=0))
        mixed_low = jnp.concatenate(mixed, axis=1).astype(BF16)
        left[2 * sl + 1, 1] = mixed_low

        rows_left(2 * sl + 1).start()

        @pl.when(core != sl)
        def _():
            came_act.wait_recv()

        stream = stream + act_s[sl][0:1, 0:1] * dot(mixed_low, wout_s[sl, 1], (1, 0))
        low = stream.astype(BF16)
        outs[sl] = low

        @pl.when(core != sl)
        def _():
            out_copy(sl).start()

        @pl.when(sl == 0)
        def _():
            @pl.when(first)
            def _():
                skip_copy.start()

            @pl.when(jnp.logical_not(first))
            def _():
                skip_copy.wait_recv()

            stream_s[...] = low.astype(F32) + xin[1].astype(F32)

        return carry

    lax.fori_loop(0, 2, forward, 0)

    @pl.when(first)
    def _():
        act_copy.start()
        gact_copy.wait_recv()

    g_s[...] = gin[0].astype(F32)

    def backward(step, carry):
        sl = 1 - step
        g = g_s[...]
        glow = (g * act_s[sl][0:1, 0:1]).astype(BF16)
        right[2 * sl + 1, 1, :, D:] = glow
        gm = dot(glow, wout_s[sl, 1], (1, 1))
        gq, gka, gva, gkb, gvb = [], [], [], [], []
        for p in range(PAIRS):
            at = slice(128 * p, 128 * p + 128)
            vat = slice(D + 128 * p, D + 128 * p + 128)
            qa, ka, va = window_backward(
                split_heads(gm[:HALF, at]), q2_s[sl, 1, p, :TOK], kv_s[sl, 1, :, at], kv_s[sl, 1, :, vat],
                probs_s[sl, 1, p, :TOK],
            )
            qb, kb, vb = window_backward(
                split_heads(gm[HALF:, at]), q2_s[sl, 1, p, TOK:], kv_s[sl, 2, :, at], kv_s[sl, 2, :, vat],
                probs_s[sl, 1, p, TOK:],
            )
            gq.append(jnp.concatenate([qa, qb], axis=0))
            gka.append(ka)
            gva.append(va)
            gkb.append(kb)
            gvb.append(vb)
        pair_a = jnp.concatenate(gka + gva, axis=1)
        pair_b = jnp.concatenate(gkb + gvb, axis=1)
        rim[sl, 0] = pair_a[:HALF].astype(BF16)
        rim[sl, 1] = pair_b[HALF:].astype(BF16)
        to_prev, to_next = rim_prev(sl), rim_next(sl)
        start_pair(to_prev, to_next)
        query_low = jnp.concatenate(gq, axis=1).astype(BF16)
        right[2 * sl + 1, 0, :, :D] = query_low
        part = dot(query_low, wqkv_s[sl, 1, :, :D], (1, 1))

        @pl.when(step == 1)
        def _():
            weight_term(2)

        arrive_pair(to_prev, to_next)
        pairs_low = jnp.concatenate(
            [pair_a[HALF:] + rim_in[sl, 0].astype(F32), pair_b[:HALF] + rim_in[sl, 1].astype(F32)], axis=0
        ).astype(BF16)
        right[2 * sl + 1, 0, :, D:] = pairs_low[:, :D]
        right[2 * sl + 1, 1, :, :D] = pairs_low[:, D:]

        rows_right(2 * sl + 1).start()
        part = part + dot(pairs_low, wqkv_s[sl, 1, :, D:], (1, 1))
        g = g + norm_back(xs[sl, 1], invs[sl, 1][:, 0:1], part)

        glow = g.astype(BF16)
        right[2 * sl, 1, :, D:] = glow
        gm = dot(glow, wout_s[sl, 0], (1, 1))
        gq, gk, gv = [], [], []
        for p in range(PAIRS):
            at = slice(128 * p, 128 * p + 128)
            vat = slice(D + 128 * p, D + 128 * p + 128)
            q, k, v = window_backward(
                split_heads(gm[:, at]), q2_s[sl, 0, p], kv_s[sl, 0, :, at], kv_s[sl, 0, :, vat], probs_s[sl, 0, p]
            )
            gq.append(q)
            gk.append(k)
            gv.append(v)
        low = jnp.concatenate(gq + gk + gv, axis=1).astype(BF16)
        right[2 * sl, 0] = low[:, : 2 * D]
        right[2 * sl, 1, :, :D] = low[:, 2 * D :]

        rows_right(2 * sl).start()
        part = dot(low, wqkv_s[sl, 0], (1, 1))
        g = g + norm_back(xs[sl, 0], invs[sl, 0][:, 0:1], part)
        grads[sl] = g

        @pl.when(core != sl)
        def _():
            grad_copy(sl).start()

        @pl.when(jnp.logical_not(first))
        def _():
            handoff[1 - step] = g.astype(BF16)

            @pl.when(step == 0)
            def _():
                gskip_copy.start()

            @pl.when(step == 1)
            def _():
                gact_copy.start()

        @pl.when(step == 0)
        def _():
            @pl.when(first)
            def _():
                gskip_copy.wait_recv()

            g_s[...] = g + gin[1].astype(F32)

        weight_term(2 * sl + 1)
        return carry

    lax.fori_loop(0, 2, backward, 0)
    weight_term(0)

    lax.fori_loop(0, 4, lambda step, carry: middle(3 - step, carry), 0)

    def finish(step, carry):
        unit = 3 - step
        owner, layer = unit // 2, lax.rem(unit, 2)
        fin_s[owner, layer] = last(unit)

        @pl.when(owner != core)
        def _():
            fin_copy(layer).start()

        return carry

    lax.fori_loop(0, 4, finish, 0)
    for layer in range(MAXL):
        fin_copy(layer).wait_recv()
        term_ref[layer, core] = fin_s[core, layer]
        term_ref[layer, 1 - core] = fin_in[layer]

    out_copy(core).wait_recv()
    grad_copy(core).wait_recv()
    out_ref[core] = outs[core]
    out_ref[1 - core] = out_in[...]
    grad_ref[core] = grads[core]
    grad_ref[1 - core] = grad_in[...]

    sent_act.wait_send()

    for layer in range(MAXL):
        for copy in sent_w(layer):
            copy.wait_send()
        fin_copy(layer).wait_send()
    for unit in range(4):
        rows_left(unit).wait_send()
        rows_right(unit).wait_send()
        for hop in range(1, lon_total):
            part_copy(unit, hop).wait_send()

        def sent(hop, carry):
            mid_copy(unit, hop).wait_send()
            return carry

        lax.fori_loop(1, lat_total, sent, 0)
    out_copy(1 - core).wait_send()
    grad_copy(1 - core).wait_send()
    for sl in range(2):
        left_pair(halo_prev(sl), halo_next(sl))
        left_pair(rim_prev(sl), rim_next(sl))

    @pl.when(first)
    def _():
        act_copy.wait_send()
        skip_copy.wait_send()

    @pl.when(jnp.logical_not(first))
    def _():
        gact_copy.wait_send()
        gskip_copy.wait_send()


def network(fields, cotangent, active, w_qkv, w_out, lat_total, lon_total):
    piece = 2 * D // (lat_total * lon_total)
    vmem = pl.BlockSpec(memory_space=pltpu.VMEM)
    hbm = pl.BlockSpec(memory_space=pl.ANY)
    dma = pltpu.SemaphoreType.DMA
    scratch = [
        pltpu.VMEM((2, MAXL, D, 3 * D), BF16),
        pltpu.VMEM((2, MAXL, D, D), BF16),
        pltpu.VMEM((2, 8, 128), F32),
        pltpu.VMEM((2, TOK, D), BF16),
        pltpu.VMEM((2, TOK, D), BF16),
        pltpu.VMEM((TOK, D), F32),
        pltpu.VMEM((TOK, D), F32),
        pltpu.VMEM((2, TOK, D), BF16),
        pltpu.VMEM((TOK, D), BF16),
        pltpu.VMEM((2, TOK, D), F32),
        pltpu.VMEM((TOK, D), F32),
        pltpu.VMEM((2, TOK, D), BF16),
        pltpu.VMEM((2, 2, HALF, D), BF16),
        pltpu.VMEM((2, 2, HALF, D), BF16),
        pltpu.VMEM((2, 2, HALF, 2 * D), BF16),
        pltpu.VMEM((2, 2, HALF, 2 * D), BF16),
        pltpu.VMEM((2, MAXL, TOK, D), F32),
        pltpu.VMEM((2, MAXL, TOK, 128), F32),
        pltpu.VMEM((2, MAXL, PAIRS, 2 * TOK, TOK), F32),
        pltpu.VMEM((2, MAXL, PAIRS, 2 * TOK, 128), BF16),
        pltpu.VMEM((2, 3, TOK, 2 * D), BF16),
        pltpu.VMEM((4, 2, TOK, D), BF16),
        pltpu.VMEM((4, 2, TOK, D), BF16),
        pltpu.VMEM((4, 2, TOK, 2 * D), BF16),
        pltpu.VMEM((4, TOK, 2 * D), BF16),
        pltpu.VMEM((4, lon_total, lat_total, piece, D), BF16),
        pltpu.VMEM((4, lon_total - 1, lat_total, piece, D), BF16),
        pltpu.VMEM((4, lat_total, piece, D), BF16),
        pltpu.VMEM((4, lat_total - 1, piece, D), BF16),
        pltpu.VMEM((2, MAXL, piece, D), F32),
        pltpu.VMEM((MAXL, piece, D), F32),
        dma((MAXL, 2)),
        dma((MAXL, 2)),
        dma((MAXL, 2)),
        dma((2,)),
        dma((2,)),
        dma((2,)),
        dma((2,)),
        dma((2,)),
        dma,
        dma,
        dma,
        dma,
        dma((2, 2)),
        dma((2, 2)),
        dma((2, 2)),
        dma((2, 2)),
        dma((4,)),
        dma((4,)),
        dma((4,)),
        dma((4,)),
        dma((4, lon_total - 1)),
        dma((4, lon_total - 1)),
        dma((4, lat_total - 1)),
        dma((4, lat_total - 1)),
        dma((MAXL,)),
        dma((MAXL,)),
    ]
    return pl.pallas_call(
        partial(body, lat_total, lon_total),
        out_shape=(
            jax.ShapeDtypeStruct((2, TOK, D), BF16),
            jax.ShapeDtypeStruct((2, TOK, D), F32),
            jax.ShapeDtypeStruct((MAXL, 2, piece, D), F32),
        ),
        in_specs=[vmem, vmem, vmem, hbm, hbm],
        out_specs=(vmem, vmem, vmem),
        scratch_shapes=scratch,
        compiler_params=pltpu.CompilerParams(
            collective_id=0, has_side_effects=True, vmem_limit_bytes=56 * 1024 * 1024
        ),
        name="network",
    )(fields, cotangent, active, w_qkv, w_out)


def to_rows(cells, core):
    pair = lax.dynamic_slice_in_dim(cells, 2 * core, 2, axis=0)
    return pair.reshape(WIN_LEV, 2, 6, WIN_LON, D).transpose(1, 0, 2, 3, 4).reshape(TOK, D)


def from_rows(rows):
    shaped = rows.reshape(2, 2, WIN_LEV, 6, WIN_LON, D).transpose(0, 2, 1, 3, 4, 5)
    return shaped.reshape(1, 2 * WIN_LEV, 12, WIN_LON, D)


def local(fields, cotangent, depths, w_qkv, w_out):
    core = lax.rem(lax.axis_index("segment"), 2)
    active = jnp.broadcast_to((depths[0] > 1).astype(F32), (8, 128))
    out_rows, grad_rows, terms = network(
        to_rows(fields, core), to_rows(cotangent, core), active, w_qkv[0], w_out[0],
        lax.axis_size("lat"), lax.axis_size("lon"),
    )
    shaped = terms.reshape(MAXL, 4, -1, D).transpose(0, 2, 1, 3).reshape(MAXL, -1, 4 * D)
    return (
        from_rows(out_rows),
        from_rows(grad_rows),
        shaped[None, :, :, : 3 * D],
        shaped[None, :, :, 3 * D :],
    )


def solution(mesh):
    placed = (
        P(None, "lat", "lon", None),
        P(None, "lat", "lon", None),
        P("segment"),
        P("segment", None, None, None),
        P("segment", None, None, None),
    )
    return jax.shard_map(
        local,
        mesh=mesh,
        in_specs=placed,
        out_specs=(
            P("segment", None, "lat", "lon", None),
            P("segment", None, "lat", "lon", None),
            P("segment", None, ("lat", "lon"), None),
            P("segment", None, ("lat", "lon"), None),
        ),
        check_vma=False,
    )
```

```python
from functools import partial

import jax
import jax.numpy as jnp
from jax import lax
from jax.experimental import pallas as pl
from jax.experimental.pallas import tpu as pltpu
from jax.sharding import PartitionSpec as P

HEADS = 8
HS = 64
WIN_LEV = 2
WIN_LON = 6
MAXL = 2
D = 512
PAIRS = 4
HALF = 72
TOK = 144
EPSILON = 1e-05
MESH = pl.DeviceIdType.MESH
F32 = jnp.float32
BF16 = jnp.bfloat16


def dot(a, b, contract):
    return lax.dot_general(a, b, ((contract[:1], contract[1:]), ((), ())), preferred_element_type=F32)


def normalize(stream):
    center = stream - jnp.mean(stream, axis=-1, keepdims=True)
    inverse = lax.rsqrt(jnp.mean(center * center, axis=-1, keepdims=True) + EPSILON)
    return (center * inverse, inverse)


def norm_back(scaled, inverse, gradient):
    middle = gradient - jnp.mean(gradient, axis=-1, keepdims=True)
    return inverse * (middle - scaled * jnp.mean(gradient * scaled, axis=-1, keepdims=True))


def split_heads(value):
    low = lax.broadcasted_iota(jnp.int32, value.shape, 1) < HS
    return jnp.concatenate([jnp.where(low, value, 0.0), jnp.where(low, 0.0, value)], axis=0).astype(BF16)


def join_heads(value):
    count = value.shape[0] // 2
    low = lax.broadcasted_iota(jnp.int32, (count, value.shape[1]), 1) < HS
    return jnp.where(low, value[:count], value[count:])


def window_forward(q2, k, v, valid):
    exponent = jnp.exp(dot(q2, k, (1, 1)) * (HS ** -0.5))
    if valid is not None:
        exponent = exponent * valid
    probs = exponent * (1.0 / jnp.sum(exponent, axis=-1, keepdims=True))
    return probs, join_heads(dot(probs.astype(BF16), v, (1, 0)))


def window_backward(gm2, q2, k, v, probs):
    grad_probs = dot(gm2, v, (1, 1))
    inner = jnp.sum(probs * grad_probs, axis=-1, keepdims=True)
    grad_scores = (probs * (grad_probs - inner) * (HS ** -0.5)).astype(BF16)
    gq = dot(grad_scores, k, (1, 0))
    gk = dot(grad_scores, q2, (0, 0))
    gv = dot(probs.astype(BF16), gm2, (0, 0))
    return gq, gk, gv


def body(
    lat_total, lon_total,
    fields_ref, cot_ref, depth_ref, wqkv_hbm, wout_hbm,
    out_ref, grad_ref, qkv_ref, wo_ref,
    wqkv_s, wout_s, act_s, stage, xin, gin, stream_s, g_s, outs, out_in, grads, grad_in, handoff,
    nrm, halo, rim, rim_in, xs, invs, probs_s, q2_s, kv_s, left, left_in, right, right_in,
    part_s, one_in, one_s, two_in, two_s, three_in, col_s, col_in, fin_s, fin_in,
    own_sem, w_send, w_recv, a_sem, i_sem, x_send, x_recv, g_send, g_recv, o_send, o_recv, s_send, s_recv,
    h_send, h_recv, r_send, r_recv, l_send, l_recv, t_send, t_recv,
    p_send, p_recv, z_send, z_recv, f_send, f_recv,
):
    seg = lax.axis_index("segment")
    lat = lax.axis_index("lat")
    lon = lax.axis_index("lon")
    core = lax.rem(seg, 2)
    first = seg < 2
    high = lax.rem(lat, 2)
    z_at = lat // 2
    z_total = lat_total // 2
    at_home = core == high
    has_far = jnp.where(core == 0, lat > 1, lat < lat_total - 2)
    other = seg + 1 - 2 * core
    partner = {"segment": other, "lat": lat, "lon": lon}
    across = {"segment": lax.rem(seg + 2, 4), "lat": lat, "lon": lon}
    beyond = {"segment": other, "lat": lax.rem(lat + lat_total - 2 + 4 * core, lat_total), "lon": lon}
    twin_lat = lat + 1 - 2 * high
    twin = {"segment": seg, "lat": twin_lat, "lon": lon}
    diagonal = {"segment": other, "lat": twin_lat, "lon": lon}

    def remote(src, dst, send, recv, to):
        return pltpu.make_async_remote_copy(
            src_ref=src, dst_ref=dst, send_sem=send, recv_sem=recv, device_id=to, device_id_type=MESH
        )

    barrier = pltpu.get_barrier_semaphore()
    pl.semaphore_signal(barrier, inc=1, device_id=partner, device_id_type=MESH)
    pl.semaphore_signal(barrier, inc=1, device_id=across, device_id_type=MESH)
    pl.semaphore_signal(barrier, inc=1, device_id=diagonal, device_id_type=MESH)

    @pl.when(has_far)
    def _():
        pl.semaphore_signal(barrier, inc=1, device_id=beyond, device_id_type=MESH)

    side, end = lax.rem((lon + 1) // 2, 2), lon // 2
    lon_side = lon + 1 - 2 * lax.rem(lon, 2)
    lon_end = lon_total - 1 - lon
    flat = core == 0
    peer_one = {"segment": seg, "lat": jnp.where(flat, lat, twin_lat), "lon": jnp.where(flat, lon_side, lon)}
    peer_two = {"segment": seg, "lat": lat, "lon": lon_end}
    peer_three = {"segment": seg, "lat": jnp.where(flat, twin_lat, lat), "lon": jnp.where(flat, lon, lon_side)}
    at_one = jnp.where(flat, side, high)
    at_three = jnp.where(flat, high, side)
    pl.semaphore_signal(barrier, inc=1, device_id=peer_one, device_id_type=MESH)
    pl.semaphore_signal(barrier, inc=1, device_id=peer_two, device_id_type=MESH)
    pl.semaphore_signal(barrier, inc=1, device_id=peer_three, device_id_type=MESH)

    def z_peer(hop):
        return {"segment": seg, "lat": lax.rem(lat + 2 * hop, lat_total), "lon": lon}

    def greet_z(hop, carry):
        pl.semaphore_signal(barrier, inc=1, device_id=z_peer(hop), device_id_type=MESH)
        return carry

    lax.fori_loop(1, z_total, greet_z, 0)

    def own_w(layer):
        return (
            pltpu.make_async_copy(wqkv_hbm.at[layer], wqkv_s.at[core, layer], own_sem.at[layer, 0]),
            pltpu.make_async_copy(wout_hbm.at[layer], wout_s.at[core, layer], own_sem.at[layer, 1]),
        )

    def sent_w(layer):
        return (
            remote(wqkv_hbm.at[layer], wqkv_s.at[core, layer], w_send.at[layer, 0], w_recv.at[layer, 0], partner),
            remote(wout_hbm.at[layer], wout_s.at[core, layer], w_send.at[layer, 1], w_recv.at[layer, 1], partner),
        )

    def came_w(layer):
        other = 1 - core
        return (
            remote(wqkv_hbm.at[layer], wqkv_s.at[other, layer], w_send.at[layer, 0], w_recv.at[layer, 0], partner),
            remote(wout_hbm.at[layer], wout_s.at[other, layer], w_send.at[layer, 1], w_recv.at[layer, 1], partner),
        )

    for layer in range(MAXL):
        for copy in own_w(layer):
            copy.start()

    act_s[core] = jnp.broadcast_to((depth_ref[0] > 1).astype(F32), (8, 128))

    zeros = jnp.zeros((2, HALF, D), BF16)

    @pl.when(first)
    def _():
        xin[1] = zeros

        @pl.when(at_home)
        def _():
            xin[0, 0] = fields_ref[high, 1 - core]
            xin[0, 1] = fields_ref[high, core]
            stage[0] = fields_ref[1 - high, 1 - core]
            stage[1] = fields_ref[1 - high, core]

    @pl.when(jnp.logical_not(first))
    def _():
        gin[1] = zeros

        @pl.when(at_home)
        def _():
            gin[0, 0] = cot_ref[high, 1 - core]
            gin[0, 1] = cot_ref[high, core]
            stage[0] = cot_ref[1 - high, 1 - core]
            stage[1] = cot_ref[1 - high, core]

    @pl.when(jnp.logical_not(has_far))
    def _():
        for sl in range(2):
            halo[sl, 1] = jnp.zeros((HALF, D), BF16)
            rim_in[sl, 1] = jnp.zeros((HALF, 2 * D), BF16)

    pl.semaphore_wait(barrier, 6 + z_total - 1 + has_far.astype(jnp.int32))

    sent_act = remote(act_s.at[core], act_s.at[core], a_sem.at[0], a_sem.at[1], partner)
    came_act = remote(act_s.at[core], act_s.at[1 - core], a_sem.at[0], a_sem.at[1], partner)
    field_copy = remote(stage, xin.at[0], i_sem.at[0], i_sem.at[1], twin)
    target_copy = remote(stage, gin.at[0], i_sem.at[2], i_sem.at[3], twin)

    @pl.when(jnp.logical_and(at_home, first))
    def _():
        field_copy.start()

    @pl.when(jnp.logical_and(at_home, jnp.logical_not(first)))
    def _():
        target_copy.start()

    sent_act.start()
    for layer in range(MAXL):
        for copy in sent_w(layer):
            copy.start()

    def halo_near(sl):
        return remote(nrm.at[sl, 0], halo.at[sl, 0], h_send.at[sl, 0], h_recv.at[sl, 0], partner)

    def halo_far(sl):
        return remote(nrm.at[sl, 1], halo.at[sl, 1], h_send.at[sl, 1], h_recv.at[sl, 1], beyond)

    def rim_near(sl):
        return remote(rim.at[sl, 0], rim_in.at[sl, 0], r_send.at[sl, 0], r_recv.at[sl, 0], partner)

    def rim_far(sl):
        return remote(rim.at[sl, 1], rim_in.at[sl, 1], r_send.at[sl, 1], r_recv.at[sl, 1], beyond)

    def start_far(copy):
        @pl.when(has_far)
        def _():
            copy.start()

    def arrive_far(copy):
        @pl.when(has_far)
        def _():
            copy.wait_recv()

    def rows_left(unit):
        return remote(left.at[unit], left_in.at[unit], l_send.at[unit], l_recv.at[unit], partner)

    def rows_right(unit):
        return remote(right.at[unit, 1 - core], right_in.at[unit], t_send.at[unit], t_recv.at[unit], partner)

    def one_copy(unit):
        return remote(part_s.at[unit, 1 - at_one], one_in.at[unit], p_send.at[unit, 0], p_recv.at[unit, 0], peer_one)

    def two_copy(unit):
        return remote(one_s.at[unit, 1 - end], two_in.at[unit], p_send.at[unit, 1], p_recv.at[unit, 1], peer_two)

    def three_copy(unit):
        return remote(two_s.at[unit, 1 - at_three], three_in.at[unit], p_send.at[unit, 2], p_recv.at[unit, 2], peer_three)

    def col_copy(unit, hop):
        return remote(
            col_s.at[unit, lax.rem(z_at + hop, z_total)], col_in.at[unit, hop - 1],
            z_send.at[unit, hop - 1], z_recv.at[unit, hop - 1], z_peer(hop),
        )

    def fin_copy(layer):
        return remote(fin_s.at[1 - core, layer], fin_in.at[layer], f_send.at[layer], f_recv.at[layer], partner)

    def weight_term(unit):
        rows_left(unit).wait_recv()
        rows_right(unit).wait_recv()
        normed = jnp.concatenate([left[unit, 0], left_in[unit, 0]], axis=0)
        second = jnp.concatenate([left[unit, core], left_in[unit, core]], axis=0)
        grads_low = jnp.concatenate([right[unit, core], right_in[unit]], axis=0)
        shape = (z_total, 2, lon_total, D // (lat_total * lon_total), D)
        one = dot(normed, grads_low[:, :D], (0, 0)).reshape(shape)
        two = dot(second, grads_low[:, D:], (0, 0)).reshape(shape)
        both = jnp.concatenate([one, two], axis=3).astype(BF16)
        for x in range(2):
            for to in range(lon_total):
                to_side, to_end = (to + 1) // 2 % 2, to // 2
                part_s[unit, jnp.where(flat, to_side, x), to_end, jnp.where(flat, x, to_side)] = both[:, x, to]

        @pl.when(first)
        def _():
            one_copy(unit).start()

    def stage_two(unit):
        one_copy(unit).wait_recv()
        one_s[unit] = (part_s[unit, at_one].astype(F32) + one_in[unit].astype(F32)).astype(BF16)
        two_copy(unit).start()

    def stage_three(unit):
        two_copy(unit).wait_recv()
        two_s[unit] = (one_s[unit, end].astype(F32) + two_in[unit].astype(F32)).astype(BF16)
        three_copy(unit).start()

    def stage_four(unit):
        three_copy(unit).wait_recv()
        col_s[unit] = (two_s[unit, at_three].astype(F32) + three_in[unit].astype(F32)).astype(BF16)

        def send(hop, carry):
            col_copy(unit, hop).start()
            return carry

        lax.fori_loop(1, z_total, send, 0)

    def stage_five(unit):
        def add(hop, total):
            col_copy(unit, hop).wait_recv()
            return total + col_in[unit, hop - 1].astype(F32)

        owner, layer = unit // 2, unit % 2
        fin_s[owner, layer] = lax.fori_loop(1, z_total, add, col_s[unit, z_at].astype(F32))

        @pl.when(owner != core)
        def _():
            fin_copy(layer).start()

    act_copy = remote(outs.at[1], xin.at[0], x_send.at[0], x_recv.at[0], across)
    skip_copy = remote(outs.at[0], xin.at[1], x_send.at[1], x_recv.at[1], across)
    gact_copy = remote(handoff.at[0], gin.at[0], g_send.at[0], g_recv.at[0], across)
    gskip_copy = remote(handoff.at[1], gin.at[1], g_send.at[1], g_recv.at[1], across)

    def owner_of(sl):
        return {"segment": seg - core + sl, "lat": lat - high + core, "lon": lon}

    def out_copy(sl):
        return remote(outs.at[sl], out_in.at[high], o_send.at[sl], o_recv.at[high], owner_of(sl))

    def grad_copy(sl):
        return remote(grads.at[sl], grad_in.at[high], s_send.at[sl], s_recv.at[high], owner_of(sl))

    def hand_over(sl, copy, target, source):
        mine = jnp.logical_and(at_home, core == sl)

        @pl.when(mine)
        def _():
            target[high] = source[sl]

        @pl.when(jnp.logical_not(mine))
        def _():
            copy.start()

    key_at = lax.broadcasted_iota(jnp.int32, (1, TOK), 1)
    valid_far = jnp.where(key_at < HALF, 1.0, has_far.astype(F32))

    def rows_of(ref, index):
        return jnp.concatenate([ref[index, 0].astype(F32), ref[index, 1].astype(F32)], axis=0)

    def weights_ready(sl, layer):
        @pl.when(core == sl)
        def _():
            for copy in own_w(layer):
                copy.wait()

        @pl.when(core != sl)
        def _():
            for copy in came_w(layer):
                copy.wait_recv()

    @pl.when(jnp.logical_not(first))
    def _():
        act_copy.wait_recv()

    @pl.when(jnp.logical_and(first, jnp.logical_not(at_home)))
    def _():
        field_copy.wait_recv()

    stream_s[...] = rows_of(xin, 0)

    def forward(sl, carry):
        stream = stream_s[...]
        scaled, inverse = normalize(stream)
        normed = scaled.astype(BF16)
        xs[sl, 0] = scaled
        invs[sl, 0] = jnp.broadcast_to(inverse, (TOK, 128))
        left[2 * sl, 0] = normed
        weights_ready(sl, 0)
        qkv = dot(normed, wqkv_s[sl, 0], (1, 0))
        kv_low = qkv[:, D:].astype(BF16)
        kv_s[sl, 0] = kv_low

        def attend(layer, part, qkv, keys, valid):
            mixed = []
            for p in range(PAIRS):
                at = slice(128 * p, 128 * p + 128)
                q2 = split_heads(qkv[HALF * part : HALF * part + HALF, at])
                q2_s[sl, layer, p, TOK * part : TOK * part + TOK] = q2
                probs, mix = window_forward(q2, keys[:, at], keys[:, D + 128 * p : D + 128 * p + 128], valid)
                probs_s[sl, layer, p, TOK * part : TOK * part + TOK] = probs
                mixed.append(mix)
            return jnp.concatenate(mixed, axis=1)

        mixed = [None, None]
        streams = [None, None]
        scales = [None, None]
        for part in (1, 0):
            rows = slice(HALF * part, HALF * part + HALF)
            mixed[part] = attend(0, part, qkv, kv_low, None)
            streams[part] = stream[rows] + dot(mixed[part].astype(BF16), wout_s[sl, 0], (1, 0))
            scaled, inverse = normalize(streams[part])
            nrm[sl, part] = scaled.astype(BF16)
            xs[sl, 1, rows] = scaled
            invs[sl, 1, rows] = jnp.broadcast_to(inverse, (HALF, 128))
            scales[part] = scaled
            if part == 1:
                start_far(halo_far(sl))
            else:
                halo_near(sl).start()
        left[2 * sl, 1] = jnp.concatenate(mixed, axis=0).astype(BF16)
        stream = jnp.concatenate(streams, axis=0)

        normed = jnp.concatenate(scales, axis=0).astype(BF16)
        left[2 * sl + 1, 0] = normed
        weights_ready(sl, 1)

        rows_left(2 * sl).start()
        qkv = dot(normed, wqkv_s[sl, 1], (1, 0))
        for part in (0, 1):
            if part == 0:
                halo_near(sl).wait_recv()
            else:
                arrive_far(halo_far(sl))
            beside = dot(halo[sl, part], wqkv_s[sl, 1, :, D:], (1, 0))
            keys = jnp.concatenate([qkv[HALF * part : HALF * part + HALF, D:], beside], axis=0).astype(BF16)
            kv_s[sl, 1 + part] = keys
            mixed[part] = attend(1, part, qkv, keys, valid_far if part == 1 else None)
        mixed_low = jnp.concatenate(mixed, axis=0).astype(BF16)
        left[2 * sl + 1, 1] = mixed_low

        rows_left(2 * sl + 1).start()

        @pl.when(core != sl)
        def _():
            came_act.wait_recv()

        stream = stream + act_s[sl][0:1, 0:1] * dot(mixed_low, wout_s[sl, 1], (1, 0))
        for part in range(2):
            outs[sl, part] = stream[HALF * part : HALF * part + HALF].astype(BF16)
        hand_over(sl, out_copy(sl), out_in, outs)

        @pl.when(sl == 0)
        def _():
            @pl.when(first)
            def _():
                skip_copy.start()

            @pl.when(jnp.logical_not(first))
            def _():
                skip_copy.wait_recv()

            stream_s[...] = stream.astype(BF16).astype(F32) + rows_of(xin, 1)

        return carry

    lax.fori_loop(0, 2, forward, 0)

    @pl.when(first)
    def _():
        act_copy.start()
        gact_copy.wait_recv()

    @pl.when(jnp.logical_not(jnp.logical_or(first, at_home)))
    def _():
        target_copy.wait_recv()

    g_s[...] = rows_of(gin, 0)

    def backward(step, carry):
        sl = 1 - step
        g = g_s[...]
        glow = (g * act_s[sl][0:1, 0:1]).astype(BF16)
        right[2 * sl + 1, 1, :, D:] = glow
        gm = dot(glow, wout_s[sl, 1], (1, 1))
        gq, pairs = [None, None], [None, None]
        for part in (1, 0):
            rows = slice(TOK * part, TOK * part + TOK)
            q, k, v = [], [], []
            for p in range(PAIRS):
                at = slice(128 * p, 128 * p + 128)
                vat = slice(D + 128 * p, D + 128 * p + 128)
                found = window_backward(
                    split_heads(gm[HALF * part : HALF * part + HALF, at]), q2_s[sl, 1, p, rows],
                    kv_s[sl, 1 + part, :, at], kv_s[sl, 1 + part, :, vat], probs_s[sl, 1, p, rows],
                )
                q.append(join_heads(found[0]))
                k.append(found[1])
                v.append(found[2])
            gq[part] = jnp.concatenate(q, axis=1)
            pairs[part] = jnp.concatenate(k + v, axis=1)
            rim[sl, part] = pairs[part][HALF:].astype(BF16)
            if part == 1:
                start_far(rim_far(sl))
            else:
                rim_near(sl).start()
        query_low = jnp.concatenate(gq, axis=0).astype(BF16)
        right[2 * sl + 1, 0, :, :D] = query_low
        part = dot(query_low, wqkv_s[sl, 1, :, :D], (1, 1))

        @pl.when(step == 1)
        def _():
            weight_term(2)

        rim_near(sl).wait_recv()
        arrive_far(rim_far(sl))
        pairs_low = jnp.concatenate(
            [pairs[part][:HALF] + rim_in[sl, part].astype(F32) for part in range(2)], axis=0
        ).astype(BF16)
        right[2 * sl + 1, 0, :, D:] = pairs_low[:, :D]
        right[2 * sl + 1, 1, :, :D] = pairs_low[:, D:]

        rows_right(2 * sl + 1).start()
        part = part + dot(pairs_low, wqkv_s[sl, 1, :, D:], (1, 1))
        g = g + norm_back(xs[sl, 1], invs[sl, 1][:, 0:1], part)

        glow = g.astype(BF16)
        right[2 * sl, 1, :, D:] = glow
        gm = dot(glow, wout_s[sl, 0], (1, 1))
        gq, gk, gv = [], [], []
        for p in range(PAIRS):
            at = slice(128 * p, 128 * p + 128)
            vat = slice(D + 128 * p, D + 128 * p + 128)
            gm2 = jnp.concatenate([split_heads(gm[:HALF, at]), split_heads(gm[HALF:, at])], axis=0)
            q, k, v = window_backward(
                gm2, q2_s[sl, 0, p], kv_s[sl, 0, :, at], kv_s[sl, 0, :, vat], probs_s[sl, 0, p]
            )
            gq.append(jnp.concatenate([join_heads(q[:TOK]), join_heads(q[TOK:])], axis=0))
            gk.append(k)
            gv.append(v)
        low = jnp.concatenate(gq + gk + gv, axis=1).astype(BF16)
        right[2 * sl, 0] = low[:, : 2 * D]
        right[2 * sl, 1, :, :D] = low[:, 2 * D :]

        rows_right(2 * sl).start()
        part = dot(low, wqkv_s[sl, 0], (1, 1))
        g = g + norm_back(xs[sl, 0], invs[sl, 0][:, 0:1], part)
        for part in range(2):
            grads[sl, part] = g[HALF * part : HALF * part + HALF]
        @pl.when(step == 0)
        def _():
            hand_over(sl, grad_copy(sl), grad_in, grads)

        @pl.when(jnp.logical_not(first))
        def _():
            for part in range(2):
                handoff[1 - step, part] = g[HALF * part : HALF * part + HALF].astype(BF16)

            @pl.when(step == 0)
            def _():
                gskip_copy.start()

            @pl.when(step == 1)
            def _():
                gact_copy.start()

        @pl.when(step == 0)
        def _():
            @pl.when(first)
            def _():
                gskip_copy.wait_recv()

            g_s[...] = g + rows_of(gin, 1)

        weight_term(2 * sl + 1)
        return carry

    lax.fori_loop(0, 2, backward, 0)
    weight_term(0)

    @pl.when(jnp.logical_not(first))
    def _():
        for unit in (3, 2, 1, 0):
            one_copy(unit).start()

    hand_over(0, grad_copy(0), grad_in, grads)
    stage_two(3)
    stage_two(2)
    stage_three(3)
    stage_two(1)
    stage_three(2)
    stage_four(3)
    stage_three(1)
    stage_four(2)
    stage_two(0)
    stage_four(1)
    stage_five(3)
    stage_five(2)
    stage_three(0)
    stage_five(1)
    stage_four(0)
    stage_five(0)

    for pair in range(2):
        came = jnp.logical_not(jnp.logical_and(at_home, high == pair))

        @pl.when(came)
        def _():
            remote(outs.at[0], out_in.at[pair], o_send.at[0], o_recv.at[pair], partner).wait_recv()
            remote(grads.at[0], grad_in.at[pair], s_send.at[0], s_recv.at[pair], partner).wait_recv()

        out_ref[pair, 0] = out_in[pair, 1 - high]
        out_ref[pair, 1] = out_in[pair, high]
        grad_ref[pair, 0] = grad_in[pair, 1 - high]
        grad_ref[pair, 1] = grad_in[pair, high]

    piece = D // (lat_total * lon_total)
    for layer in range(MAXL):
        fin_copy(layer).wait_recv()
        mine, came = fin_s[core, layer], fin_in[layer]
        first_half = jnp.where(core == 0, mine, came)
        second_half = jnp.where(core == 0, came, mine)
        qkv_ref[layer, :, :D] = first_half[:piece]
        qkv_ref[layer, :, D : 2 * D] = first_half[piece:]
        qkv_ref[layer, :, 2 * D :] = second_half[:piece]
        wo_ref[layer] = second_half[piece:]

    sent_act.wait_send()

    for layer in range(MAXL):
        for copy in sent_w(layer):
            copy.wait_send()
        fin_copy(layer).wait_send()
    for unit in range(4):
        rows_left(unit).wait_send()
        rows_right(unit).wait_send()

        one_copy(unit).wait_send()
        two_copy(unit).wait_send()
        three_copy(unit).wait_send()

        def sent(hop, carry):
            col_copy(unit, hop).wait_send()
            return carry

        lax.fori_loop(1, z_total, sent, 0)
    for sl in range(2):
        @pl.when(jnp.logical_not(jnp.logical_and(at_home, core == sl)))
        def _():
            out_copy(sl).wait_send()
            grad_copy(sl).wait_send()

        halo_near(sl).wait_send()
        rim_near(sl).wait_send()

        @pl.when(has_far)
        def _():
            halo_far(sl).wait_send()
            rim_far(sl).wait_send()

    @pl.when(jnp.logical_and(at_home, first))
    def _():
        field_copy.wait_send()

    @pl.when(jnp.logical_and(at_home, jnp.logical_not(first)))
    def _():
        target_copy.wait_send()

    @pl.when(first)
    def _():
        act_copy.wait_send()
        skip_copy.wait_send()

    @pl.when(jnp.logical_not(first))
    def _():
        gact_copy.wait_send()
        gskip_copy.wait_send()


def network(fields, cotangent, depths, w_qkv, w_out, lat_total, lon_total):
    piece = 2 * D // (lat_total * lon_total)
    z_total = lat_total // 2
    vmem = pl.BlockSpec(memory_space=pltpu.VMEM)
    hbm = pl.BlockSpec(memory_space=pl.ANY)
    dma = pltpu.SemaphoreType.DMA
    scratch = [
        pltpu.VMEM((2, MAXL, D, 3 * D), BF16),
        pltpu.VMEM((2, MAXL, D, D), BF16),
        pltpu.VMEM((2, 8, 128), F32),
        pltpu.VMEM((2, HALF, D), BF16),
        pltpu.VMEM((2, 2, HALF, D), BF16),
        pltpu.VMEM((2, 2, HALF, D), BF16),
        pltpu.VMEM((TOK, D), F32),
        pltpu.VMEM((TOK, D), F32),
        pltpu.VMEM((2, 2, HALF, D), BF16),
        pltpu.VMEM((2, 2, HALF, D), BF16),
        pltpu.VMEM((2, 2, HALF, D), F32),
        pltpu.VMEM((2, 2, HALF, D), F32),
        pltpu.VMEM((2, 2, HALF, D), BF16),
        pltpu.VMEM((2, 2, HALF, D), BF16),
        pltpu.VMEM((2, 2, HALF, D), BF16),
        pltpu.VMEM((2, 2, HALF, 2 * D), BF16),
        pltpu.VMEM((2, 2, HALF, 2 * D), BF16),
        pltpu.VMEM((2, MAXL, TOK, D), F32),
        pltpu.VMEM((2, MAXL, TOK, 128), F32),
        pltpu.VMEM((2, MAXL, PAIRS, 2 * TOK, TOK), F32),
        pltpu.VMEM((2, MAXL, PAIRS, 2 * TOK, 128), BF16),
        pltpu.VMEM((2, 3, TOK, 2 * D), BF16),
        pltpu.VMEM((4, 2, TOK, D), BF16),
        pltpu.VMEM((4, 2, TOK, D), BF16),
        pltpu.VMEM((4, 2, TOK, 2 * D), BF16),
        pltpu.VMEM((4, TOK, 2 * D), BF16),
        pltpu.VMEM((4, 2, 2, 2, z_total, piece, D), BF16),
        pltpu.VMEM((4, 2, 2, z_total, piece, D), BF16),
        pltpu.VMEM((4, 2, 2, z_total, piece, D), BF16),
        pltpu.VMEM((4, 2, z_total, piece, D), BF16),
        pltpu.VMEM((4, 2, z_total, piece, D), BF16),
        pltpu.VMEM((4, z_total, piece, D), BF16),
        pltpu.VMEM((4, z_total, piece, D), BF16),
        pltpu.VMEM((4, z_total - 1, piece, D), BF16),
        pltpu.VMEM((2, MAXL, piece, D), F32),
        pltpu.VMEM((MAXL, piece, D), F32),
        dma((MAXL, 2)),
        dma((MAXL, 2)),
        dma((MAXL, 2)),
        dma((2,)),
        dma((4,)),
        dma((2,)),
        dma((2,)),
        dma((2,)),
        dma((2,)),
        dma((2,)),
        dma((2,)),
        dma((2,)),
        dma((2,)),
        dma((2, 2)),
        dma((2, 2)),
        dma((2, 2)),
        dma((2, 2)),
        dma((4,)),
        dma((4,)),
        dma((4,)),
        dma((4,)),
        dma((4, 3)),
        dma((4, 3)),
        dma((4, z_total - 1)),
        dma((4, z_total - 1)),
        dma((MAXL,)),
        dma((MAXL,)),
    ]
    return pl.pallas_call(
        partial(body, lat_total, lon_total),
        out_shape=(
            jax.ShapeDtypeStruct((2, 2, HALF, D), BF16),
            jax.ShapeDtypeStruct((2, 2, HALF, D), F32),
            jax.ShapeDtypeStruct((MAXL, piece // 2, 3 * D), F32),
            jax.ShapeDtypeStruct((MAXL, piece // 2, D), F32),
        ),
        in_specs=[vmem, vmem, pl.BlockSpec(memory_space=pltpu.SMEM), hbm, hbm],
        out_specs=(vmem, vmem, vmem, vmem),
        scratch_shapes=scratch,
        compiler_params=pltpu.CompilerParams(
            collective_id=0, has_side_effects=True, vmem_limit_bytes=56 * 1024 * 1024
        ),
        name="network",
    )(fields, cotangent, depths, w_qkv, w_out)


def to_rows(cells):
    shaped = cells.reshape(2, WIN_LEV, 2, 6, WIN_LON, D).transpose(0, 2, 1, 3, 4, 5)
    return shaped.reshape(2, 2, HALF, D)


def from_rows(rows):
    shaped = rows.reshape(2, 2, WIN_LEV, 6, WIN_LON, D).transpose(0, 2, 1, 3, 4, 5)
    return shaped.reshape(1, 2 * WIN_LEV, 12, WIN_LON, D)


def local(fields, cotangent, depths, w_qkv, w_out):
    out_rows, grad_rows, qkv_grad, out_grad = network(
        to_rows(fields), to_rows(cotangent), depths, w_qkv[0], w_out[0],
        lax.axis_size("lat"), lax.axis_size("lon"),
    )
    return (
        from_rows(out_rows),
        from_rows(grad_rows),
        qkv_grad[None],
        out_grad[None],
    )


def solution(mesh):
    placed = (
        P(None, "lat", "lon", None),
        P(None, "lat", "lon", None),
        P("segment"),
        P("segment", None, None, None),
        P("segment", None, None, None),
    )
    return jax.shard_map(
        local,
        mesh=mesh,
        in_specs=placed,
        out_specs=(
            P("segment", None, "lat", "lon", None),
            P("segment", None, "lat", "lon", None),
            P("segment", None, ("lat", "lon"), None),
            P("segment", None, ("lat", "lon"), None),
        ),
        check_vma=False,
    )
```

```python
from functools import partial

import jax
import jax.numpy as jnp
from jax import lax
from jax.experimental import pallas as pl
from jax.experimental.pallas import tpu as pltpu
from jax.sharding import PartitionSpec as P

HEADS = 8
HS = 64
WIN_LEV = 2
WIN_LON = 6
MAXL = 2
D = 512
PAIRS = 4
HALF = 72
TOK = 144
EPSILON = 1e-05
MESH = pl.DeviceIdType.MESH
F32 = jnp.float32
BF16 = jnp.bfloat16


def dot(a, b, contract):
    return lax.dot_general(a, b, ((contract[:1], contract[1:]), ((), ())), preferred_element_type=F32)


def normalize(stream):
    center = stream - jnp.mean(stream, axis=-1, keepdims=True)
    inverse = lax.rsqrt(jnp.mean(center * center, axis=-1, keepdims=True) + EPSILON)
    return (center * inverse, inverse)


def norm_back(scaled, inverse, gradient):
    middle = gradient - jnp.mean(gradient, axis=-1, keepdims=True)
    return inverse * (middle - scaled * jnp.mean(gradient * scaled, axis=-1, keepdims=True))


def split_heads(value):
    low = lax.broadcasted_iota(jnp.int32, value.shape, 1) < HS
    return jnp.concatenate([jnp.where(low, value, 0.0), jnp.where(low, 0.0, value)], axis=0).astype(BF16)


def join_heads(value):
    count = value.shape[0] // 2
    low = lax.broadcasted_iota(jnp.int32, (count, value.shape[1]), 1) < HS
    return jnp.where(low, value[:count], value[count:])


def window_forward(q2, k, v, valid):
    exponent = jnp.exp(dot(k, q2, (1, 1)) * (HS ** -0.5))
    if valid is not None:
        exponent = exponent * valid
    probs = exponent * (1.0 / jnp.sum(exponent, axis=0, keepdims=True))
    return probs, join_heads(dot(probs.astype(BF16), v, (0, 0)))


def window_backward(gm2, q2, k, v, probs):
    grad_probs = dot(v, gm2, (1, 1))
    inner = jnp.sum(probs * grad_probs, axis=0, keepdims=True)
    grad_scores = (probs * (grad_probs - inner) * (HS ** -0.5)).astype(BF16)
    gq = join_heads(dot(grad_scores, k, (0, 0)))
    gk = dot(grad_scores, q2, (1, 0))
    gv = dot(probs.astype(BF16), gm2, (1, 0))
    return gq, gk, gv


def picker(pair, shape, row_dim):
    rows = lax.broadcasted_iota(jnp.int32, shape, row_dim)
    cells = lax.broadcasted_iota(jnp.int32, shape, 1 - row_dim)
    return jnp.where(cells == 4 * (rows // 2) + 2 * pair + rows % 2, 1.0, 0.0)


def take_rows(ref, pair, half):
    cells = [ref[6 * half + row, col].astype(F32) for row in range(6) for col in range(WIN_LON)]
    cells = jnp.concatenate(cells, axis=0).astype(BF16)
    return dot(picker(pair, (HALF, TOK), 0).astype(BF16), cells, (1, 0)).astype(BF16)


def put_rows(ref, half, pairs):
    cells = 0.0
    for pair in range(2):
        cells = cells + lax.dot_general(
            picker(pair, (TOK, HALF), 1), pairs[pair], (((1,), (0,)), ((), ())),
            precision=lax.Precision.HIGHEST, preferred_element_type=F32,
        )
    for row in range(6):
        for col in range(WIN_LON):
            at = 4 * (WIN_LON * row + col)
            ref[6 * half + row, col] = cells[at : at + 4].astype(ref.dtype)


def body(
    lat_total, lon_total,
    fields_ref, cot_ref, depth_ref, wqkv_hbm, wout_hbm,
    out_ref, grad_ref, qkv_ref, wo_ref,
    wqkv_s, wout_s, act_s, stage, xin, gin, stream_s, g_s, outs, out_in, grads, grad_in, handoff,
    nrm, halo, rim, rim_in, xs, invs, probs_s, q2_s, kv_s, left, left_in, right, right_in,
    part_s, one_in, one_s, two_in, two_s, three_in, col_s, col_in, fin_s, fin_in,
    own_sem, w_send, w_recv, a_sem, i_sem, x_send, x_recv, g_send, g_recv, o_send, o_recv, s_send, s_recv,
    h_send, h_recv, r_send, r_recv, l_send, l_recv, t_send, t_recv,
    p_send, p_recv, z_send, z_recv, f_send, f_recv,
):
    seg = lax.axis_index("segment")
    lat = lax.axis_index("lat")
    lon = lax.axis_index("lon")
    core = lax.rem(seg, 2)
    first = seg < 2
    high = lax.rem(lat, 2)
    z_at = lat // 2
    z_total = lat_total // 2
    at_home = core == high
    has_far = jnp.where(core == 0, lat > 1, lat < lat_total - 2)
    other = seg + 1 - 2 * core
    partner = {"segment": other, "lat": lat, "lon": lon}
    across = {"segment": lax.rem(seg + 2, 4), "lat": lat, "lon": lon}
    beyond = {"segment": other, "lat": lax.rem(lat + lat_total - 2 + 4 * core, lat_total), "lon": lon}
    twin_lat = lat + 1 - 2 * high
    twin = {"segment": seg, "lat": twin_lat, "lon": lon}
    diagonal = {"segment": other, "lat": twin_lat, "lon": lon}

    def remote(src, dst, send, recv, to):
        return pltpu.make_async_remote_copy(
            src_ref=src, dst_ref=dst, send_sem=send, recv_sem=recv, device_id=to, device_id_type=MESH
        )

    barrier = pltpu.get_barrier_semaphore()
    pl.semaphore_signal(barrier, inc=1, device_id=partner, device_id_type=MESH)
    pl.semaphore_signal(barrier, inc=1, device_id=across, device_id_type=MESH)
    pl.semaphore_signal(barrier, inc=1, device_id=diagonal, device_id_type=MESH)

    @pl.when(has_far)
    def _():
        pl.semaphore_signal(barrier, inc=1, device_id=beyond, device_id_type=MESH)

    side, end = lax.rem((lon + 1) // 2, 2), lon // 2
    lon_side = lon + 1 - 2 * lax.rem(lon, 2)
    lon_end = lon_total - 1 - lon
    for peer_lon in (lon_side, lon_end):
        to = {"segment": seg, "lat": lat, "lon": peer_lon}
        pl.semaphore_signal(barrier, inc=1, device_id=to, device_id_type=MESH)
    pl.semaphore_signal(barrier, inc=1, device_id=twin, device_id_type=MESH)

    def z_peer(hop):
        return {"segment": seg, "lat": lax.rem(lat + 2 * hop, lat_total), "lon": lon}

    def greet_z(hop, carry):
        pl.semaphore_signal(barrier, inc=1, device_id=z_peer(hop), device_id_type=MESH)
        return carry

    lax.fori_loop(1, z_total, greet_z, 0)

    def own_w(layer):
        return (
            pltpu.make_async_copy(wqkv_hbm.at[layer], wqkv_s.at[core, layer], own_sem.at[layer, 0]),
            pltpu.make_async_copy(wout_hbm.at[layer], wout_s.at[core, layer], own_sem.at[layer, 1]),
        )

    def sent_w(layer):
        return (
            remote(wqkv_hbm.at[layer], wqkv_s.at[core, layer], w_send.at[layer, 0], w_recv.at[layer, 0], partner),
            remote(wout_hbm.at[layer], wout_s.at[core, layer], w_send.at[layer, 1], w_recv.at[layer, 1], partner),
        )

    def came_w(layer):
        other = 1 - core
        return (
            remote(wqkv_hbm.at[layer], wqkv_s.at[other, layer], w_send.at[layer, 0], w_recv.at[layer, 0], partner),
            remote(wout_hbm.at[layer], wout_s.at[other, layer], w_send.at[layer, 1], w_recv.at[layer, 1], partner),
        )

    for layer in range(MAXL):
        for copy in own_w(layer):
            copy.start()

    act_s[core] = jnp.broadcast_to((depth_ref[0] > 1).astype(F32), (8, 128))

    zeros = jnp.zeros((2, HALF, D), BF16)

    @pl.when(first)
    def _():
        xin[1] = zeros

        @pl.when(at_home)
        def _():
            xin[0, 0] = take_rows(fields_ref, high, 1 - core)
            xin[0, 1] = take_rows(fields_ref, high, core)
            stage[0] = take_rows(fields_ref, 1 - high, 1 - core)
            stage[1] = take_rows(fields_ref, 1 - high, core)

    @pl.when(jnp.logical_not(first))
    def _():
        gin[1] = zeros

        @pl.when(at_home)
        def _():
            gin[0, 0] = take_rows(cot_ref, high, 1 - core)
            gin[0, 1] = take_rows(cot_ref, high, core)
            stage[0] = take_rows(cot_ref, 1 - high, 1 - core)
            stage[1] = take_rows(cot_ref, 1 - high, core)

    @pl.when(jnp.logical_not(has_far))
    def _():
        for sl in range(2):
            halo[sl, 1] = jnp.zeros((HALF, D), BF16)
            rim_in[sl, 1] = jnp.zeros((HALF, 2 * D), BF16)

    pl.semaphore_wait(barrier, 6 + z_total - 1 + has_far.astype(jnp.int32))

    sent_act = remote(act_s.at[core], act_s.at[core], a_sem.at[0], a_sem.at[1], partner)
    came_act = remote(act_s.at[core], act_s.at[1 - core], a_sem.at[0], a_sem.at[1], partner)
    field_copy = remote(stage, xin.at[0], i_sem.at[0], i_sem.at[1], twin)
    target_copy = remote(stage, gin.at[0], i_sem.at[2], i_sem.at[3], twin)

    @pl.when(jnp.logical_and(at_home, first))
    def _():
        field_copy.start()

    @pl.when(jnp.logical_and(at_home, jnp.logical_not(first)))
    def _():
        target_copy.start()

    sent_act.start()
    for layer in range(MAXL):
        for copy in sent_w(layer):
            copy.start()

    def halo_near(sl):
        return remote(nrm.at[sl, 0], halo.at[sl, 0], h_send.at[sl, 0], h_recv.at[sl, 0], partner)

    def halo_far(sl):
        return remote(nrm.at[sl, 1], halo.at[sl, 1], h_send.at[sl, 1], h_recv.at[sl, 1], beyond)

    def rim_near(sl):
        return remote(rim.at[sl, 0], rim_in.at[sl, 0], r_send.at[sl, 0], r_recv.at[sl, 0], partner)

    def rim_far(sl):
        return remote(rim.at[sl, 1], rim_in.at[sl, 1], r_send.at[sl, 1], r_recv.at[sl, 1], beyond)

    def start_far(copy):
        @pl.when(has_far)
        def _():
            copy.start()

    def arrive_far(copy):
        @pl.when(has_far)
        def _():
            copy.wait_recv()

    def rows_left(unit):
        return remote(left.at[unit], left_in.at[unit], l_send.at[unit], l_recv.at[unit], partner)

    def rows_right(unit):
        return remote(right.at[unit, 1 - core], right_in.at[unit], t_send.at[unit], t_recv.at[unit], partner)

    def order_of(unit, tile):
        if tile == 0:
            return core == 1, core == 0
        return jnp.logical_and(core == 1, unit == 0), jnp.logical_and(core == 1, lax.rem(unit, 2) == 1)

    def arranged(unit, tile, of_side, of_end, of_twin):
        twin_first, side_first = order_of(unit, tile)
        if tile == 0:
            return jnp.where(twin_first, of_twin, of_side), of_end, jnp.where(twin_first, of_side, of_twin)
        one = jnp.where(twin_first, of_twin, jnp.where(side_first, of_side, of_end))
        return one, jnp.where(side_first, of_end, of_side), jnp.where(twin_first, of_end, of_twin)

    def pairs_of(unit, tile):
        ats = arranged(unit, tile, side, end, high)
        lats = arranged(unit, tile, lat, lat, twin_lat)
        lons = arranged(unit, tile, lon_side, lon_end, lon)
        return [(at, {"segment": seg, "lat": a, "lon": b}) for at, a, b in zip(ats, lats, lons)]

    def pair_copy(unit, tile, level):
        at, peer = pairs_of(unit, tile)[level]
        source = (part_s, one_s, two_s)[level].at[unit, tile, 1 - at]
        target = (one_in, two_in, three_in)[level].at[unit, tile]
        return remote(source, target, p_send.at[unit, tile, level], p_recv.at[unit, tile, level], peer)

    def pair_sum(unit, tile, level):
        at = pairs_of(unit, tile)[level][0]
        pair_copy(unit, tile, level).wait_recv()
        kept = (part_s, one_s, two_s)[level][unit, tile, at]
        return (kept.astype(F32) + (one_in, two_in, three_in)[level][unit, tile].astype(F32)).astype(BF16)

    def col_copy(unit, hop):
        return remote(
            col_s.at[unit, lax.rem(z_at + hop, z_total)], col_in.at[unit, hop - 1],
            z_send.at[unit, hop - 1], z_recv.at[unit, hop - 1], z_peer(hop),
        )

    def fin_copy(layer):
        return remote(fin_s.at[1 - core, layer], fin_in.at[layer], f_send.at[layer], f_recv.at[layer], partner)

    def weight_term(unit):
        rows_left(unit).wait_recv()
        rows_right(unit).wait_recv()
        normed = jnp.concatenate([left[unit, 0], left_in[unit, 0]], axis=0)
        second = jnp.concatenate([left[unit, core], left_in[unit, core]], axis=0)
        grads_low = jnp.concatenate([right[unit, core], right_in[unit]], axis=0)
        shape = (z_total, 2, lon_total, D // (lat_total * lon_total), D)
        for tile in range(2):
            term = dot(second if tile else normed, grads_low[:, D * tile : D * tile + D], (0, 0)).reshape(shape)
            term = jnp.concatenate([term[..., : D // 2], term[..., D // 2 :]], axis=3).astype(BF16)
            for x in range(2):
                for to in range(lon_total):
                    to_side, to_end = (to + 1) // 2 % 2, to // 2
                    one, two, three = arranged(unit, tile, to_side, to_end, x)
                    part_s[unit, tile, one, two, three] = term[:, x, to]

            @pl.when(first)
            def _():
                pair_copy(unit, tile, 0).start()

    def stage_two(unit):
        for tile in range(2):
            one_s[unit, tile] = pair_sum(unit, tile, 0)
            pair_copy(unit, tile, 1).start()

    def stage_three(unit):
        for tile in range(2):
            two_s[unit, tile] = pair_sum(unit, tile, 1)
            pair_copy(unit, tile, 2).start()

    def stage_four(unit):
        for tile in range(2):
            col_s[unit, :, tile] = pair_sum(unit, tile, 2)

        for hop in sorted(range(1, z_total), key=lambda hop: -min(hop, z_total - hop)):
            col_copy(unit, hop).start()

    def stage_five(unit):
        def add(hop, total):
            col_copy(unit, hop).wait_recv()
            return total + col_in[unit, hop - 1].astype(F32)

        owner, layer = unit // 2, unit % 2
        fin_s[owner, layer] = lax.fori_loop(1, z_total, add, col_s[unit, z_at].astype(F32))

        @pl.when(owner != core)
        def _():
            fin_copy(layer).start()

    act_copy = remote(outs.at[1], xin.at[0], x_send.at[0], x_recv.at[0], across)
    skip_copy = remote(outs.at[0], xin.at[1], x_send.at[1], x_recv.at[1], across)
    gact_copy = remote(handoff.at[0], gin.at[0], g_send.at[0], g_recv.at[0], across)
    gskip_copy = remote(handoff.at[1], gin.at[1], g_send.at[1], g_recv.at[1], across)

    def owner_of(sl):
        return {"segment": seg - core + sl, "lat": lat - high + core, "lon": lon}

    def out_copy(sl):
        return remote(outs.at[sl], out_in.at[high], o_send.at[sl], o_recv.at[high], owner_of(sl))

    def grad_copy(sl):
        return remote(grads.at[sl], grad_in.at[high], s_send.at[sl], s_recv.at[high], owner_of(sl))

    def hand_over(sl, copy, target, source):
        mine = jnp.logical_and(at_home, core == sl)

        @pl.when(mine)
        def _():
            target[high] = source[sl]

        @pl.when(jnp.logical_not(mine))
        def _():
            copy.start()

    key_at = lax.broadcasted_iota(jnp.int32, (TOK, 1), 0)
    valid_far = jnp.where(key_at < HALF, 1.0, has_far.astype(F32))

    def rows_of(ref, index):
        return jnp.concatenate([ref[index, 0].astype(F32), ref[index, 1].astype(F32)], axis=0)

    def weights_ready(sl, layer):
        @pl.when(core == sl)
        def _():
            for copy in own_w(layer):
                copy.wait()

        @pl.when(core != sl)
        def _():
            for copy in came_w(layer):
                copy.wait_recv()

    @pl.when(jnp.logical_not(first))
    def _():
        act_copy.wait_recv()

    @pl.when(jnp.logical_and(first, jnp.logical_not(at_home)))
    def _():
        field_copy.wait_recv()

    stream_s[...] = rows_of(xin, 0)

    def forward(sl, carry):
        stream = stream_s[...]
        scaled, inverse = normalize(stream)
        normed = scaled.astype(BF16)
        xs[sl, 0] = scaled
        invs[sl, 0] = jnp.broadcast_to(inverse, (TOK, 128))
        left[2 * sl, 0] = normed
        weights_ready(sl, 0)
        qkv = dot(normed, wqkv_s[sl, 0], (1, 0))
        kv_low = qkv[:, D:].astype(BF16)
        kv_s[sl, 0] = kv_low

        def attend(layer, part, qkv, keys, valid):
            mixed = []
            for p in range(PAIRS):
                at = slice(128 * p, 128 * p + 128)
                q2 = split_heads(qkv[HALF * part : HALF * part + HALF, at])
                q2_s[sl, layer, p, TOK * part : TOK * part + TOK] = q2
                probs, mix = window_forward(q2, keys[:, at], keys[:, D + 128 * p : D + 128 * p + 128], valid)
                probs_s[sl, layer, p, part] = probs
                mixed.append(mix)
            return jnp.concatenate(mixed, axis=1)

        mixed = [None, None]
        streams = [None, None]
        scales = [None, None]
        for part in (1, 0):
            rows = slice(HALF * part, HALF * part + HALF)
            mixed[part] = attend(0, part, qkv, kv_low, None)
            streams[part] = stream[rows] + dot(mixed[part].astype(BF16), wout_s[sl, 0], (1, 0))
            scaled, inverse = normalize(streams[part])
            nrm[sl, part] = scaled.astype(BF16)
            xs[sl, 1, rows] = scaled
            invs[sl, 1, rows] = jnp.broadcast_to(inverse, (HALF, 128))
            scales[part] = scaled
            if part == 1:
                start_far(halo_far(sl))
            else:
                halo_near(sl).start()
        left[2 * sl, 1] = jnp.concatenate(mixed, axis=0).astype(BF16)
        stream = jnp.concatenate(streams, axis=0)

        normed = jnp.concatenate(scales, axis=0).astype(BF16)
        left[2 * sl + 1, 0] = normed
        weights_ready(sl, 1)

        rows_left(2 * sl).start()
        qkv = dot(normed, wqkv_s[sl, 1], (1, 0))
        for part in (0, 1):
            if part == 0:
                halo_near(sl).wait_recv()
            else:
                arrive_far(halo_far(sl))
            beside = dot(halo[sl, part], wqkv_s[sl, 1, :, D:], (1, 0))
            keys = jnp.concatenate([qkv[HALF * part : HALF * part + HALF, D:], beside], axis=0).astype(BF16)
            kv_s[sl, 1 + part] = keys
            mixed[part] = attend(1, part, qkv, keys, valid_far if part == 1 else None)
        mixed_low = jnp.concatenate(mixed, axis=0).astype(BF16)
        left[2 * sl + 1, 1] = mixed_low

        rows_left(2 * sl + 1).start()

        @pl.when(core != sl)
        def _():
            came_act.wait_recv()

        stream = stream + act_s[sl][0:1, 0:1] * dot(mixed_low, wout_s[sl, 1], (1, 0))
        for part in range(2):
            outs[sl, part] = stream[HALF * part : HALF * part + HALF].astype(BF16)
        hand_over(sl, out_copy(sl), out_in, outs)

        @pl.when(sl == 0)
        def _():
            @pl.when(first)
            def _():
                skip_copy.start()

            @pl.when(jnp.logical_not(first))
            def _():
                skip_copy.wait_recv()

            stream_s[...] = stream.astype(BF16).astype(F32) + rows_of(xin, 1)

        return carry

    lax.fori_loop(0, 2, forward, 0)

    @pl.when(first)
    def _():
        act_copy.start()
        gact_copy.wait_recv()

    @pl.when(jnp.logical_not(jnp.logical_or(first, at_home)))
    def _():
        target_copy.wait_recv()

    g_s[...] = rows_of(gin, 0)

    def backward(step, carry):
        sl = 1 - step
        g = g_s[...]
        glow = (g * act_s[sl][0:1, 0:1]).astype(BF16)
        right[2 * sl + 1, 1, :, D:] = glow
        gm = dot(glow, wout_s[sl, 1], (1, 1))
        gq, pairs = [None, None], [None, None]
        for part in (1, 0):
            rows = slice(TOK * part, TOK * part + TOK)
            q, k, v = [], [], []
            for p in range(PAIRS):
                at = slice(128 * p, 128 * p + 128)
                vat = slice(D + 128 * p, D + 128 * p + 128)
                found = window_backward(
                    split_heads(gm[HALF * part : HALF * part + HALF, at]), q2_s[sl, 1, p, rows],
                    kv_s[sl, 1 + part, :, at], kv_s[sl, 1 + part, :, vat], probs_s[sl, 1, p, part],
                )
                q.append(found[0])
                k.append(found[1])
                v.append(found[2])
            gq[part] = jnp.concatenate(q, axis=1)
            pairs[part] = jnp.concatenate(k + v, axis=1)
            rim[sl, part] = pairs[part][HALF:].astype(BF16)
            if part == 1:
                start_far(rim_far(sl))
            else:
                rim_near(sl).start()
        query_low = jnp.concatenate(gq, axis=0).astype(BF16)
        right[2 * sl + 1, 0, :, :D] = query_low
        part = dot(query_low, wqkv_s[sl, 1, :, :D], (1, 1))

        @pl.when(step == 1)
        def _():
            weight_term(2)

        rim_near(sl).wait_recv()
        arrive_far(rim_far(sl))
        pairs_low = jnp.concatenate(
            [pairs[part][:HALF] + rim_in[sl, part].astype(F32) for part in range(2)], axis=0
        ).astype(BF16)
        right[2 * sl + 1, 0, :, D:] = pairs_low[:, :D]
        right[2 * sl + 1, 1, :, :D] = pairs_low[:, D:]

        rows_right(2 * sl + 1).start()
        part = part + dot(pairs_low, wqkv_s[sl, 1, :, D:], (1, 1))
        g = g + norm_back(xs[sl, 1], invs[sl, 1][:, 0:1], part)

        glow = g.astype(BF16)
        right[2 * sl, 1, :, D:] = glow
        gm = dot(glow, wout_s[sl, 0], (1, 1))
        gq, gk, gv = [], [], []
        for p in range(PAIRS):
            at = slice(128 * p, 128 * p + 128)
            vat = slice(D + 128 * p, D + 128 * p + 128)
            found = [
                window_backward(
                    split_heads(gm[HALF * part : HALF * part + HALF, at]), q2_s[sl, 0, p, TOK * part : TOK * part + TOK],
                    kv_s[sl, 0, :, at], kv_s[sl, 0, :, vat], probs_s[sl, 0, p, part],
                )
                for part in range(2)
            ]
            gq.append(jnp.concatenate([found[0][0], found[1][0]], axis=0))
            k = found[0][1] + found[1][1]
            v = found[0][2] + found[1][2]
            gk.append(k)
            gv.append(v)
        low = jnp.concatenate(gq + gk + gv, axis=1).astype(BF16)
        right[2 * sl, 0] = low[:, : 2 * D]
        right[2 * sl, 1, :, :D] = low[:, 2 * D :]

        rows_right(2 * sl).start()
        part = dot(low, wqkv_s[sl, 0], (1, 1))
        g = g + norm_back(xs[sl, 0], invs[sl, 0][:, 0:1], part)
        for part in range(2):
            grads[sl, part] = g[HALF * part : HALF * part + HALF]
        @pl.when(step == 0)
        def _():
            hand_over(sl, grad_copy(sl), grad_in, grads)

        @pl.when(jnp.logical_not(first))
        def _():
            for part in range(2):
                handoff[1 - step, part] = g[HALF * part : HALF * part + HALF].astype(BF16)

            @pl.when(step == 0)
            def _():
                gskip_copy.start()

            @pl.when(step == 1)
            def _():
                gact_copy.start()

        @pl.when(step == 0)
        def _():
            @pl.when(first)
            def _():
                gskip_copy.wait_recv()

            g_s[...] = g + rows_of(gin, 1)

        weight_term(2 * sl + 1)
        return carry

    lax.fori_loop(0, 2, backward, 0)
    weight_term(0)

    @pl.when(jnp.logical_not(first))
    def _():
        for unit in (3, 2, 1, 0):
            for tile in range(2):
                pair_copy(unit, tile, 0).start()

    hand_over(0, grad_copy(0), grad_in, grads)
    stage_two(3)
    stage_two(2)
    stage_three(3)
    stage_two(1)
    stage_three(2)
    stage_four(3)
    stage_three(1)
    stage_four(2)
    stage_two(0)
    stage_four(1)
    stage_five(3)
    stage_five(2)
    stage_three(0)
    stage_five(1)
    for pair in range(2):
        came = jnp.logical_not(jnp.logical_and(at_home, high == pair))

        @pl.when(came)
        def _():
            remote(outs.at[0], out_in.at[pair], o_send.at[0], o_recv.at[pair], partner).wait_recv()
            remote(grads.at[0], grad_in.at[pair], s_send.at[0], s_recv.at[pair], partner).wait_recv()

    for half in range(2):
        index = (1 - high) if half == 0 else high
        put_rows(out_ref, half, [out_in[pair, index].astype(F32) for pair in range(2)])
        put_rows(grad_ref, half, [grad_in[pair, index] for pair in range(2)])

    stage_four(0)
    stage_five(0)

    piece = D // (lat_total * lon_total)
    for layer in range(MAXL):
        fin_copy(layer).wait_recv()
        mine, came = fin_s[core, layer], fin_in[layer]
        first_half = jnp.where(core == 0, mine, came)
        second_half = jnp.where(core == 0, came, mine)
        for side_at in range(2):
            at = D // 2 * side_at
            rows = slice(piece * side_at, piece * side_at + piece)
            qkv_ref[layer, :, at : at + D // 2] = first_half[0, rows]
            qkv_ref[layer, :, D + at : D + at + D // 2] = first_half[1, rows]
            qkv_ref[layer, :, 2 * D + at : 2 * D + at + D // 2] = second_half[0, rows]
            wo_ref[layer, :, at : at + D // 2] = second_half[1, rows]

    sent_act.wait_send()

    for layer in range(MAXL):
        for copy in sent_w(layer):
            copy.wait_send()
        fin_copy(layer).wait_send()
    for unit in range(4):
        rows_left(unit).wait_send()
        rows_right(unit).wait_send()

        for tile in range(2):
            for level in range(3):
                pair_copy(unit, tile, level).wait_send()

        def sent(hop, carry):
            col_copy(unit, hop).wait_send()
            return carry

        lax.fori_loop(1, z_total, sent, 0)
    for sl in range(2):
        @pl.when(jnp.logical_not(jnp.logical_and(at_home, core == sl)))
        def _():
            out_copy(sl).wait_send()
            grad_copy(sl).wait_send()

        halo_near(sl).wait_send()
        rim_near(sl).wait_send()

        @pl.when(has_far)
        def _():
            halo_far(sl).wait_send()
            rim_far(sl).wait_send()

    @pl.when(jnp.logical_and(at_home, first))
    def _():
        field_copy.wait_send()

    @pl.when(jnp.logical_and(at_home, jnp.logical_not(first)))
    def _():
        target_copy.wait_send()

    @pl.when(first)
    def _():
        act_copy.wait_send()
        skip_copy.wait_send()

    @pl.when(jnp.logical_not(first))
    def _():
        gact_copy.wait_send()
        gskip_copy.wait_send()


def network(fields, cotangent, depths, w_qkv, w_out, lat_total, lon_total):
    piece = 2 * D // (lat_total * lon_total)
    z_total = lat_total // 2
    vmem = pl.BlockSpec(memory_space=pltpu.VMEM)
    hbm = pl.BlockSpec(memory_space=pl.ANY)
    dma = pltpu.SemaphoreType.DMA
    scratch = [
        pltpu.VMEM((2, MAXL, D, 3 * D), BF16),
        pltpu.VMEM((2, MAXL, D, D), BF16),
        pltpu.VMEM((2, 8, 128), F32),
        pltpu.VMEM((2, HALF, D), BF16),
        pltpu.VMEM((2, 2, HALF, D), BF16),
        pltpu.VMEM((2, 2, HALF, D), BF16),
        pltpu.VMEM((TOK, D), F32),
        pltpu.VMEM((TOK, D), F32),
        pltpu.VMEM((2, 2, HALF, D), BF16),
        pltpu.VMEM((2, 2, HALF, D), BF16),
        pltpu.VMEM((2, 2, HALF, D), F32),
        pltpu.VMEM((2, 2, HALF, D), F32),
        pltpu.VMEM((2, 2, HALF, D), BF16),
        pltpu.VMEM((2, 2, HALF, D), BF16),
        pltpu.VMEM((2, 2, HALF, D), BF16),
        pltpu.VMEM((2, 2, HALF, 2 * D), BF16),
        pltpu.VMEM((2, 2, HALF, 2 * D), BF16),
        pltpu.VMEM((2, MAXL, TOK, D), F32),
        pltpu.VMEM((2, MAXL, TOK, 128), F32),
        pltpu.VMEM((2, MAXL, PAIRS, 2, TOK, TOK), F32),
        pltpu.VMEM((2, MAXL, PAIRS, 2 * TOK, 128), BF16),
        pltpu.VMEM((2, 3, TOK, 2 * D), BF16),
        pltpu.VMEM((4, 2, TOK, D), BF16),
        pltpu.VMEM((4, 2, TOK, D), BF16),
        pltpu.VMEM((4, 2, TOK, 2 * D), BF16),
        pltpu.VMEM((4, TOK, 2 * D), BF16),
        pltpu.VMEM((4, 2, 2, 2, 2, z_total, piece, D // 2), BF16),
        pltpu.VMEM((4, 2, 2, 2, z_total, piece, D // 2), BF16),
        pltpu.VMEM((4, 2, 2, 2, z_total, piece, D // 2), BF16),
        pltpu.VMEM((4, 2, 2, z_total, piece, D // 2), BF16),
        pltpu.VMEM((4, 2, 2, z_total, piece, D // 2), BF16),
        pltpu.VMEM((4, 2, z_total, piece, D // 2), BF16),
        pltpu.VMEM((4, z_total, 2, piece, D // 2), BF16),
        pltpu.VMEM((4, z_total - 1, 2, piece, D // 2), BF16),
        pltpu.VMEM((2, MAXL, 2, piece, D // 2), F32),
        pltpu.VMEM((MAXL, 2, piece, D // 2), F32),
        dma((MAXL, 2)),
        dma((MAXL, 2)),
        dma((MAXL, 2)),
        dma((2,)),
        dma((4,)),
        dma((2,)),
        dma((2,)),
        dma((2,)),
        dma((2,)),
        dma((2,)),
        dma((2,)),
        dma((2,)),
        dma((2,)),
        dma((2, 2)),
        dma((2, 2)),
        dma((2, 2)),
        dma((2, 2)),
        dma((4,)),
        dma((4,)),
        dma((4,)),
        dma((4,)),
        dma((4, 2, 3)),
        dma((4, 2, 3)),
        dma((4, z_total - 1)),
        dma((4, z_total - 1)),
        dma((MAXL,)),
        dma((MAXL,)),
    ]
    return pl.pallas_call(
        partial(body, lat_total, lon_total),
        out_shape=(
            jax.ShapeDtypeStruct(fields.shape, BF16),
            jax.ShapeDtypeStruct(fields.shape, F32),
            jax.ShapeDtypeStruct((MAXL, piece // 2, 3 * D), F32),
            jax.ShapeDtypeStruct((MAXL, piece // 2, D), F32),
        ),
        in_specs=[vmem, vmem, pl.BlockSpec(memory_space=pltpu.SMEM), hbm, hbm],
        out_specs=(vmem, vmem, vmem, vmem),
        scratch_shapes=scratch,
        compiler_params=pltpu.CompilerParams(
            collective_id=0, has_side_effects=True, vmem_limit_bytes=56 * 1024 * 1024
        ),
        name="network",
    )(fields, cotangent, depths, w_qkv, w_out)


def local(fields, cotangent, depths, w_qkv, w_out):
    out_rows, grad_rows, qkv_grad, out_grad = network(
        fields.transpose(1, 2, 0, 3), cotangent.transpose(1, 2, 0, 3), depths, w_qkv[0], w_out[0],
        lax.axis_size("lat"), lax.axis_size("lon"),
    )
    return (
        out_rows.transpose(2, 0, 1, 3)[None],
        grad_rows.transpose(2, 0, 1, 3)[None],
        qkv_grad[None],
        out_grad[None],
    )


def solution(mesh):
    placed = (
        P(None, "lat", "lon", None),
        P(None, "lat", "lon", None),
        P("segment"),
        P("segment", None, None, None),
        P("segment", None, None, None),
    )
    return jax.shard_map(
        local,
        mesh=mesh,
        in_specs=placed,
        out_specs=(
            P("segment", None, "lat", "lon", None),
            P("segment", None, "lat", "lon", None),
            P("segment", None, ("lat", "lon"), None),
            P("segment", None, ("lat", "lon"), None),
        ),
        check_vma=False,
    )
```

```python
from functools import partial

import jax
import jax.numpy as jnp
from jax import lax
from jax.experimental import pallas as pl
from jax.experimental.pallas import tpu as pltpu
from jax.sharding import PartitionSpec as P

HEADS = 8
HS = 64
WIN_LEV = 2
WIN_LON = 6
MAXL = 2
D = 512
PAIRS = 4
HALF = 72
TOK = 144
EPSILON = 1e-05
MESH = pl.DeviceIdType.MESH
F32 = jnp.float32
BF16 = jnp.bfloat16


def dot(a, b, contract):
    return lax.dot_general(a, b, ((contract[:1], contract[1:]), ((), ())), preferred_element_type=F32)


def normalize(stream):
    center = stream - jnp.mean(stream, axis=-1, keepdims=True)
    inverse = lax.rsqrt(jnp.mean(center * center, axis=-1, keepdims=True) + EPSILON)
    return (center * inverse, inverse)


def norm_back(scaled, inverse, gradient):
    middle = gradient - jnp.mean(gradient, axis=-1, keepdims=True)
    return inverse * (middle - scaled * jnp.mean(gradient * scaled, axis=-1, keepdims=True))


def split_heads(value):
    low = lax.broadcasted_iota(jnp.int32, value.shape, 1) < HS
    return jnp.concatenate([jnp.where(low, value, 0.0), jnp.where(low, 0.0, value)], axis=0).astype(BF16)


def join_heads(value):
    count = value.shape[0] // 2
    low = lax.broadcasted_iota(jnp.int32, (count, value.shape[1]), 1) < HS
    return jnp.where(low, value[:count], value[count:])


def window_forward(q2, k, v, valid):
    exponent = jnp.exp(dot(k, q2, (1, 1)) * (HS ** -0.5))
    if valid is not None:
        exponent = exponent * valid
    probs = exponent * (1.0 / jnp.sum(exponent, axis=0, keepdims=True))
    return probs, join_heads(dot(probs.astype(BF16), v, (0, 0)))


def window_backward(gm2, q2, k, v, probs):
    grad_probs = dot(v, gm2, (1, 1))
    inner = jnp.sum(probs * grad_probs, axis=0, keepdims=True)
    grad_scores = (probs * (grad_probs - inner) * (HS ** -0.5)).astype(BF16)
    gq = join_heads(dot(grad_scores, k, (0, 0)))
    gk = dot(grad_scores, q2, (1, 0))
    gv = dot(probs.astype(BF16), gm2, (1, 0))
    return gq, gk, gv


def picker(pair, shape, row_dim):
    rows = lax.broadcasted_iota(jnp.int32, shape, row_dim)
    cells = lax.broadcasted_iota(jnp.int32, shape, 1 - row_dim)
    return jnp.where(cells == 4 * (rows // 2) + 2 * pair + rows % 2, 1.0, 0.0)


def take_rows(ref, pair, half):
    cells = [ref[6 * half + row, col].astype(F32) for row in range(6) for col in range(WIN_LON)]
    cells = jnp.concatenate(cells, axis=0).astype(BF16)
    return dot(picker(pair, (HALF, TOK), 0).astype(BF16), cells, (1, 0)).astype(BF16)


def put_rows(ref, half, pairs):
    cells = 0.0
    for pair in range(2):
        cells = cells + lax.dot_general(
            picker(pair, (TOK, HALF), 1), pairs[pair], (((1,), (0,)), ((), ())),
            precision=lax.Precision.HIGHEST, preferred_element_type=F32,
        )
    for row in range(6):
        for col in range(WIN_LON):
            at = 4 * (WIN_LON * row + col)
            ref[6 * half + row, col] = cells[at : at + 4].astype(ref.dtype)


def body(
    lat_total, lon_total,
    fields_ref, cot_ref, depth_ref, wqkv_hbm, wout_hbm,
    out_ref, grad_ref, qkv_ref, wo_ref,
    wqkv_s, wout_s, act_s, stage, xin, gin, stream_s, g_s, outs, out_in, grads, grad_in, handoff,
    nrm, halo, rim, rim_in, xs, invs, probs_s, q2_s, kv_s, left, left_in, right, right_in,
    part_s, one_in, one_s, two_in, two_s, three_in, col_s, col_in, fin_s, fin_in,
    own_sem, w_send, w_recv, a_sem, i_sem, x_send, x_recv, g_send, g_recv, o_send, o_recv, s_send, s_recv,
    h_send, h_recv, r_send, r_recv, l_send, l_recv, t_send, t_recv,
    p_send, p_recv, z_send, z_recv, f_send, f_recv,
):
    seg = lax.axis_index("segment")
    lat = lax.axis_index("lat")
    lon = lax.axis_index("lon")
    core = lax.rem(seg, 2)
    first = seg < 2
    high = lax.rem(lat, 2)
    z_at = lat // 2
    z_total = lat_total // 2
    at_home = core == high
    has_far = jnp.where(core == 0, lat > 1, lat < lat_total - 2)
    other = seg + 1 - 2 * core
    partner = {"segment": other, "lat": lat, "lon": lon}
    across = {"segment": lax.rem(seg + 2, 4), "lat": lat, "lon": lon}
    beyond = {"segment": other, "lat": lax.rem(lat + lat_total - 2 + 4 * core, lat_total), "lon": lon}
    twin_lat = lat + 1 - 2 * high
    twin = {"segment": seg, "lat": twin_lat, "lon": lon}
    diagonal = {"segment": other, "lat": twin_lat, "lon": lon}

    def remote(src, dst, send, recv, to):
        return pltpu.make_async_remote_copy(
            src_ref=src, dst_ref=dst, send_sem=send, recv_sem=recv, device_id=to, device_id_type=MESH
        )

    barrier = pltpu.get_barrier_semaphore()
    pl.semaphore_signal(barrier, inc=1, device_id=partner, device_id_type=MESH)
    pl.semaphore_signal(barrier, inc=1, device_id=across, device_id_type=MESH)
    pl.semaphore_signal(barrier, inc=1, device_id=diagonal, device_id_type=MESH)

    @pl.when(has_far)
    def _():
        pl.semaphore_signal(barrier, inc=1, device_id=beyond, device_id_type=MESH)

    side, end = lax.rem((lon + 1) // 2, 2), lon // 2
    lon_side = lon + 1 - 2 * lax.rem(lon, 2)
    lon_end = lon_total - 1 - lon
    for peer_lon in (lon_side, lon_end):
        to = {"segment": seg, "lat": lat, "lon": peer_lon}
        pl.semaphore_signal(barrier, inc=1, device_id=to, device_id_type=MESH)
    pl.semaphore_signal(barrier, inc=1, device_id=twin, device_id_type=MESH)

    def z_peer(hop):
        return {"segment": seg, "lat": lax.rem(lat + 2 * hop, lat_total), "lon": lon}

    def greet_z(hop, carry):
        pl.semaphore_signal(barrier, inc=1, device_id=z_peer(hop), device_id_type=MESH)
        return carry

    lax.fori_loop(1, z_total, greet_z, 0)

    def own_w(layer):
        return (
            pltpu.make_async_copy(wqkv_hbm.at[layer], wqkv_s.at[core, layer], own_sem.at[layer, 0]),
            pltpu.make_async_copy(wout_hbm.at[layer], wout_s.at[core, layer], own_sem.at[layer, 1]),
        )

    def sent_w(layer):
        return (
            remote(wqkv_hbm.at[layer], wqkv_s.at[core, layer], w_send.at[layer, 0], w_recv.at[layer, 0], partner),
            remote(wout_hbm.at[layer], wout_s.at[core, layer], w_send.at[layer, 1], w_recv.at[layer, 1], partner),
        )

    def came_w(layer):
        other = 1 - core
        return (
            remote(wqkv_hbm.at[layer], wqkv_s.at[other, layer], w_send.at[layer, 0], w_recv.at[layer, 0], partner),
            remote(wout_hbm.at[layer], wout_s.at[other, layer], w_send.at[layer, 1], w_recv.at[layer, 1], partner),
        )

    for layer in range(MAXL):
        for copy in own_w(layer):
            copy.start()

    act_s[core] = jnp.broadcast_to((depth_ref[0] > 1).astype(F32), (8, 128))

    zeros = jnp.zeros((2, HALF, D), BF16)

    @pl.when(first)
    def _():
        xin[1] = zeros

        @pl.when(at_home)
        def _():
            xin[0, 0] = take_rows(fields_ref, high, 1 - core)
            xin[0, 1] = take_rows(fields_ref, high, core)
            stage[0] = take_rows(fields_ref, 1 - high, 1 - core)
            stage[1] = take_rows(fields_ref, 1 - high, core)

    @pl.when(jnp.logical_not(first))
    def _():
        gin[1] = zeros

        @pl.when(at_home)
        def _():
            gin[0, 0] = take_rows(cot_ref, high, 1 - core)
            gin[0, 1] = take_rows(cot_ref, high, core)
            stage[0] = take_rows(cot_ref, 1 - high, 1 - core)
            stage[1] = take_rows(cot_ref, 1 - high, core)

    @pl.when(jnp.logical_not(has_far))
    def _():
        for sl in range(2):
            halo[sl, 1] = jnp.zeros((HALF, D), BF16)
            rim_in[sl, 1] = jnp.zeros((HALF, 2 * D), BF16)

    pl.semaphore_wait(barrier, 6 + z_total - 1 + has_far.astype(jnp.int32))

    sent_act = remote(act_s.at[core], act_s.at[core], a_sem.at[0], a_sem.at[1], partner)
    came_act = remote(act_s.at[core], act_s.at[1 - core], a_sem.at[0], a_sem.at[1], partner)
    field_copy = remote(stage, xin.at[0], i_sem.at[0], i_sem.at[1], twin)
    target_copy = remote(stage, gin.at[0], i_sem.at[2], i_sem.at[3], twin)

    @pl.when(jnp.logical_and(at_home, first))
    def _():
        field_copy.start()

    @pl.when(jnp.logical_and(at_home, jnp.logical_not(first)))
    def _():
        target_copy.start()

    sent_act.start()
    for layer in range(MAXL):
        for copy in sent_w(layer):
            copy.start()

    def halo_near(sl):
        return remote(nrm.at[sl, 0], halo.at[sl, 0], h_send.at[sl, 0], h_recv.at[sl, 0], partner)

    def halo_far(sl):
        return remote(nrm.at[sl, 1], halo.at[sl, 1], h_send.at[sl, 1], h_recv.at[sl, 1], beyond)

    def rim_near(sl):
        return remote(rim.at[sl, 0], rim_in.at[sl, 0], r_send.at[sl, 0], r_recv.at[sl, 0], partner)

    def rim_far(sl):
        return remote(rim.at[sl, 1], rim_in.at[sl, 1], r_send.at[sl, 1], r_recv.at[sl, 1], beyond)

    def start_far(copy):
        @pl.when(has_far)
        def _():
            copy.start()

    def arrive_far(copy):
        @pl.when(has_far)
        def _():
            copy.wait_recv()

    def rows_left(unit):
        return remote(left.at[unit], left_in.at[unit], l_send.at[unit], l_recv.at[unit], partner)

    def rows_right(unit):
        return remote(right.at[unit, 1 - core], right_in.at[unit], t_send.at[unit], t_recv.at[unit], partner)

    def order_of(unit, tile):
        if tile == 0:
            return core == 1, core == 0
        return jnp.logical_and(core == 1, unit == 0), jnp.logical_and(core == 1, lax.rem(unit, 2) == 1)

    def arranged(unit, tile, of_side, of_end, of_twin):
        twin_first, side_first = order_of(unit, tile)
        if tile == 0:
            return jnp.where(twin_first, of_twin, of_side), of_end, jnp.where(twin_first, of_side, of_twin)
        one = jnp.where(twin_first, of_twin, jnp.where(side_first, of_side, of_end))
        return one, jnp.where(side_first, of_end, of_side), jnp.where(twin_first, of_end, of_twin)

    def pairs_of(unit, tile):
        ats = arranged(unit, tile, side, end, high)
        lats = arranged(unit, tile, lat, lat, twin_lat)
        lons = arranged(unit, tile, lon_side, lon_end, lon)
        return [(at, {"segment": seg, "lat": a, "lon": b}) for at, a, b in zip(ats, lats, lons)]

    def pair_copy(unit, tile, level):
        at, peer = pairs_of(unit, tile)[level]
        source = (part_s, one_s, two_s)[level].at[unit, tile, 1 - at]
        target = (one_in, two_in, three_in)[level].at[unit, tile]
        return remote(source, target, p_send.at[unit, tile, level], p_recv.at[unit, tile, level], peer)

    def pair_sum(unit, tile, level):
        at = pairs_of(unit, tile)[level][0]
        pair_copy(unit, tile, level).wait_recv()
        kept = (part_s, one_s, two_s)[level][unit, tile, at]
        return (kept.astype(F32) + (one_in, two_in, three_in)[level][unit, tile].astype(F32)).astype(BF16)

    def col_copy(unit, hop):
        return remote(
            col_s.at[unit, lax.rem(z_at + hop, z_total)], col_in.at[unit, hop - 1],
            z_send.at[unit, hop - 1], z_recv.at[unit, hop - 1], z_peer(hop),
        )

    def fin_copy(layer):
        return remote(fin_s.at[1 - core, layer], fin_in.at[layer], f_send.at[layer], f_recv.at[layer], partner)

    def weight_term(unit):
        rows_left(unit).wait_recv()
        rows_right(unit).wait_recv()
        normed = jnp.concatenate([left[unit, 0], left_in[unit, 0]], axis=0)
        second = jnp.concatenate([left[unit, core], left_in[unit, core]], axis=0)
        grads_low = jnp.concatenate([right[unit, core], right_in[unit]], axis=0)
        shape = (z_total, 2, lon_total, D // (lat_total * lon_total), D)
        for tile in range(2):
            term = dot(second if tile else normed, grads_low[:, D * tile : D * tile + D], (0, 0)).reshape(shape)
            term = jnp.concatenate([term[..., : D // 2], term[..., D // 2 :]], axis=3).astype(BF16)
            for x in range(2):
                for to in range(lon_total):
                    to_side, to_end = (to + 1) // 2 % 2, to // 2
                    one, two, three = arranged(unit, tile, to_side, to_end, x)
                    part_s[unit, tile, one, two, three] = term[:, x, to]

            @pl.when(first)
            def _():
                pair_copy(unit, tile, 0).start()

    def stage_two(unit):
        for tile in range(2):
            one_s[unit, tile] = pair_sum(unit, tile, 0)
            pair_copy(unit, tile, 1).start()

    def stage_three(unit):
        for tile in range(2):
            two_s[unit, tile] = pair_sum(unit, tile, 1)
            pair_copy(unit, tile, 2).start()

    def stage_four(unit):
        for tile in range(2):
            col_s[unit, :, tile] = pair_sum(unit, tile, 2)

        for hop in sorted(range(1, z_total), key=lambda hop: -min(hop, z_total - hop)):
            col_copy(unit, hop).start()

    def stage_five(unit):
        def add(hop, total):
            col_copy(unit, hop).wait_recv()
            return total + col_in[unit, hop - 1].astype(F32)

        owner, layer = unit // 2, unit % 2
        fin_s[owner, layer] = lax.fori_loop(1, z_total, add, col_s[unit, z_at].astype(F32))

        @pl.when(owner != core)
        def _():
            fin_copy(layer).start()

    act_copy = remote(outs.at[1], xin.at[0], x_send.at[0], x_recv.at[0], across)
    skip_copy = remote(outs.at[0], xin.at[1], x_send.at[1], x_recv.at[1], across)
    gact_copy = remote(handoff.at[0], gin.at[0], g_send.at[0], g_recv.at[0], across)
    gskip_copy = remote(handoff.at[1], gin.at[1], g_send.at[1], g_recv.at[1], across)

    def owner_of(sl):
        return {"segment": seg - core + sl, "lat": lat - high + core, "lon": lon}

    def out_copy(sl):
        return remote(outs.at[sl], out_in.at[high], o_send.at[sl], o_recv.at[high], owner_of(sl))

    def grad_copy(sl):
        return remote(grads.at[sl], grad_in.at[high], s_send.at[sl], s_recv.at[high], owner_of(sl))

    def hand_over(sl, copy, target, source):
        mine = jnp.logical_and(at_home, core == sl)

        @pl.when(mine)
        def _():
            target[high] = source[sl]

        @pl.when(jnp.logical_not(mine))
        def _():
            copy.start()

    key_at = lax.broadcasted_iota(jnp.int32, (TOK, 1), 0)
    valid_far = jnp.where(key_at < HALF, 1.0, has_far.astype(F32))

    def rows_of(ref, index):
        return jnp.concatenate([ref[index, 0].astype(F32), ref[index, 1].astype(F32)], axis=0)

    def weights_ready(sl, layer):
        @pl.when(core == sl)
        def _():
            for copy in own_w(layer):
                copy.wait()

        @pl.when(core != sl)
        def _():
            for copy in came_w(layer):
                copy.wait_recv()

    @pl.when(jnp.logical_not(first))
    def _():
        act_copy.wait_recv()

    @pl.when(jnp.logical_and(first, jnp.logical_not(at_home)))
    def _():
        field_copy.wait_recv()

    stream_s[...] = rows_of(xin, 0)

    def forward(sl, carry):
        stream = stream_s[...]
        scaled, inverse = normalize(stream)
        normed = scaled.astype(BF16)
        xs[sl, 0] = scaled
        invs[sl, 0] = jnp.broadcast_to(inverse, (TOK, 128))
        left[2 * sl, 0] = normed
        weights_ready(sl, 0)
        qkv = dot(normed, wqkv_s[sl, 0], (1, 0))
        kv_low = qkv[:, D:].astype(BF16)
        kv_s[sl, 0] = kv_low

        def attend(layer, part, qkv, keys, valid):
            mixed = []
            for p in range(PAIRS):
                at = slice(128 * p, 128 * p + 128)
                q2 = split_heads(qkv[HALF * part : HALF * part + HALF, at])
                q2_s[sl, layer, p, TOK * part : TOK * part + TOK] = q2
                probs, mix = window_forward(q2, keys[:, at], keys[:, D + 128 * p : D + 128 * p + 128], valid)
                probs_s[sl, layer, p, part] = probs
                mixed.append(mix)
            return jnp.concatenate(mixed, axis=1)

        mixed = [None, None]
        streams = [None, None]
        scales = [None, None]
        for part in (1, 0):
            rows = slice(HALF * part, HALF * part + HALF)
            mixed[part] = attend(0, part, qkv, kv_low, None)
            streams[part] = stream[rows] + dot(mixed[part].astype(BF16), wout_s[sl, 0], (1, 0))
            scaled, inverse = normalize(streams[part])
            nrm[sl, part] = scaled.astype(BF16)
            xs[sl, 1, rows] = scaled
            invs[sl, 1, rows] = jnp.broadcast_to(inverse, (HALF, 128))
            scales[part] = scaled
            if part == 1:
                start_far(halo_far(sl))
            else:
                halo_near(sl).start()
        left[2 * sl, 1] = jnp.concatenate(mixed, axis=0).astype(BF16)
        stream = jnp.concatenate(streams, axis=0)

        normed = jnp.concatenate(scales, axis=0).astype(BF16)
        left[2 * sl + 1, 0] = normed
        weights_ready(sl, 1)

        rows_left(2 * sl).start()
        qkv = dot(normed, wqkv_s[sl, 1], (1, 0))
        for part in (0, 1):
            if part == 0:
                halo_near(sl).wait_recv()
            else:
                arrive_far(halo_far(sl))
            beside = dot(halo[sl, part], wqkv_s[sl, 1, :, D:], (1, 0))
            keys = jnp.concatenate([qkv[HALF * part : HALF * part + HALF, D:], beside], axis=0).astype(BF16)
            kv_s[sl, 1 + part] = keys
            mixed[part] = attend(1, part, qkv, keys, valid_far if part == 1 else None)
        mixed_low = jnp.concatenate(mixed, axis=0).astype(BF16)
        left[2 * sl + 1, 1] = mixed_low

        rows_left(2 * sl + 1).start()

        @pl.when(core != sl)
        def _():
            came_act.wait_recv()

        stream = stream + act_s[sl][0:1, 0:1] * dot(mixed_low, wout_s[sl, 1], (1, 0))
        for part in range(2):
            outs[sl, part] = stream[HALF * part : HALF * part + HALF].astype(BF16)
        hand_over(sl, out_copy(sl), out_in, outs)

        @pl.when(sl == 0)
        def _():
            @pl.when(first)
            def _():
                skip_copy.start()

            @pl.when(jnp.logical_not(first))
            def _():
                skip_copy.wait_recv()

            stream_s[...] = stream.astype(BF16).astype(F32) + rows_of(xin, 1)

        return carry

    lax.fori_loop(0, 2, forward, 0)

    @pl.when(first)
    def _():
        act_copy.start()
        gact_copy.wait_recv()

    @pl.when(jnp.logical_not(jnp.logical_or(first, at_home)))
    def _():
        target_copy.wait_recv()

    g_s[...] = rows_of(gin, 0)

    def backward(step, carry):
        sl = 1 - step
        g = g_s[...]
        glow = (g * act_s[sl][0:1, 0:1]).astype(BF16)
        right[2 * sl + 1, 1, :, D:] = glow
        gm = dot(glow, wout_s[sl, 1], (1, 1))
        gq, pairs = [None, None], [None, None]
        for part in (1, 0):
            rows = slice(TOK * part, TOK * part + TOK)
            q, k, v = [], [], []
            for p in range(PAIRS):
                at = slice(128 * p, 128 * p + 128)
                vat = slice(D + 128 * p, D + 128 * p + 128)
                found = window_backward(
                    split_heads(gm[HALF * part : HALF * part + HALF, at]), q2_s[sl, 1, p, rows],
                    kv_s[sl, 1 + part, :, at], kv_s[sl, 1 + part, :, vat], probs_s[sl, 1, p, part],
                )
                q.append(found[0])
                k.append(found[1])
                v.append(found[2])
            gq[part] = jnp.concatenate(q, axis=1)
            pairs[part] = jnp.concatenate(k + v, axis=1)
            rim[sl, part] = pairs[part][HALF:].astype(BF16)
            if part == 1:
                start_far(rim_far(sl))
            else:
                rim_near(sl).start()
        query_low = jnp.concatenate(gq, axis=0).astype(BF16)
        right[2 * sl + 1, 0, :, :D] = query_low
        part = dot(query_low, wqkv_s[sl, 1, :, :D], (1, 1))

        @pl.when(step == 1)
        def _():
            weight_term(2)

            @pl.when(first)
            def _():
                stage_two(3)

        rim_near(sl).wait_recv()
        arrive_far(rim_far(sl))
        pairs_low = jnp.concatenate(
            [pairs[part][:HALF] + rim_in[sl, part].astype(F32) for part in range(2)], axis=0
        ).astype(BF16)
        right[2 * sl + 1, 0, :, D:] = pairs_low[:, :D]
        right[2 * sl + 1, 1, :, :D] = pairs_low[:, D:]

        rows_right(2 * sl + 1).start()
        part = part + dot(pairs_low, wqkv_s[sl, 1, :, D:], (1, 1))
        g = g + norm_back(xs[sl, 1], invs[sl, 1][:, 0:1], part)

        glow = g.astype(BF16)
        right[2 * sl, 1, :, D:] = glow
        gm = dot(glow, wout_s[sl, 0], (1, 1))
        gq, gk, gv = [], [], []
        for p in range(PAIRS):
            at = slice(128 * p, 128 * p + 128)
            vat = slice(D + 128 * p, D + 128 * p + 128)
            found = [
                window_backward(
                    split_heads(gm[HALF * part : HALF * part + HALF, at]), q2_s[sl, 0, p, TOK * part : TOK * part + TOK],
                    kv_s[sl, 0, :, at], kv_s[sl, 0, :, vat], probs_s[sl, 0, p, part],
                )
                for part in range(2)
            ]
            gq.append(jnp.concatenate([found[0][0], found[1][0]], axis=0))
            k = found[0][1] + found[1][1]
            v = found[0][2] + found[1][2]
            gk.append(k)
            gv.append(v)
        low = jnp.concatenate(gq + gk + gv, axis=1).astype(BF16)
        right[2 * sl, 0] = low[:, : 2 * D]
        right[2 * sl, 1, :, :D] = low[:, 2 * D :]

        rows_right(2 * sl).start()
        part = dot(low, wqkv_s[sl, 0], (1, 1))
        g = g + norm_back(xs[sl, 0], invs[sl, 0][:, 0:1], part)
        for part in range(2):
            grads[sl, part] = g[HALF * part : HALF * part + HALF]
        @pl.when(step == 0)
        def _():
            hand_over(sl, grad_copy(sl), grad_in, grads)

        @pl.when(jnp.logical_not(first))
        def _():
            for part in range(2):
                handoff[1 - step, part] = g[HALF * part : HALF * part + HALF].astype(BF16)

            @pl.when(step == 0)
            def _():
                gskip_copy.start()

            @pl.when(step == 1)
            def _():
                gact_copy.start()

        @pl.when(step == 0)
        def _():
            @pl.when(first)
            def _():
                gskip_copy.wait_recv()

            g_s[...] = g + rows_of(gin, 1)

        weight_term(2 * sl + 1)
        return carry

    lax.fori_loop(0, 2, backward, 0)
    weight_term(0)

    @pl.when(jnp.logical_not(first))
    def _():
        for unit in (3, 2, 1, 0):
            for tile in range(2):
                pair_copy(unit, tile, 0).start()
        stage_two(3)

    hand_over(0, grad_copy(0), grad_in, grads)
    stage_two(2)
    stage_three(3)
    stage_two(1)
    stage_three(2)
    stage_two(0)
    stage_four(3)
    stage_three(1)
    stage_four(2)
    stage_three(0)
    stage_four(1)
    stage_five(3)
    for pair in range(2):
        came = jnp.logical_not(jnp.logical_and(at_home, high == pair))

        @pl.when(came)
        def _():
            remote(outs.at[0], out_in.at[pair], o_send.at[0], o_recv.at[pair], partner).wait_recv()
            remote(grads.at[0], grad_in.at[pair], s_send.at[0], s_recv.at[pair], partner).wait_recv()

    for half in range(2):
        index = (1 - high) if half == 0 else high
        put_rows(out_ref, half, [out_in[pair, index].astype(F32) for pair in range(2)])
        put_rows(grad_ref, half, [grad_in[pair, index] for pair in range(2)])

    stage_five(2)
    stage_four(0)
    stage_five(1)
    stage_five(0)

    piece = D // (lat_total * lon_total)
    for layer in range(MAXL):
        fin_copy(layer).wait_recv()
        mine, came = fin_s[core, layer], fin_in[layer]
        first_half = jnp.where(core == 0, mine, came)
        second_half = jnp.where(core == 0, came, mine)
        for side_at in range(2):
            at = D // 2 * side_at
            rows = slice(piece * side_at, piece * side_at + piece)
            qkv_ref[layer, :, at : at + D // 2] = first_half[0, rows]
            qkv_ref[layer, :, D + at : D + at + D // 2] = first_half[1, rows]
            qkv_ref[layer, :, 2 * D + at : 2 * D + at + D // 2] = second_half[0, rows]
            wo_ref[layer, :, at : at + D // 2] = second_half[1, rows]

    sent_act.wait_send()

    for layer in range(MAXL):
        for copy in sent_w(layer):
            copy.wait_send()
        fin_copy(layer).wait_send()
    for unit in range(4):
        rows_left(unit).wait_send()
        rows_right(unit).wait_send()

        for tile in range(2):
            for level in range(3):
                pair_copy(unit, tile, level).wait_send()

        def sent(hop, carry):
            col_copy(unit, hop).wait_send()
            return carry

        lax.fori_loop(1, z_total, sent, 0)
    for sl in range(2):
        @pl.when(jnp.logical_not(jnp.logical_and(at_home, core == sl)))
        def _():
            out_copy(sl).wait_send()
            grad_copy(sl).wait_send()

        halo_near(sl).wait_send()
        rim_near(sl).wait_send()

        @pl.when(has_far)
        def _():
            halo_far(sl).wait_send()
            rim_far(sl).wait_send()

    @pl.when(jnp.logical_and(at_home, first))
    def _():
        field_copy.wait_send()

    @pl.when(jnp.logical_and(at_home, jnp.logical_not(first)))
    def _():
        target_copy.wait_send()

    @pl.when(first)
    def _():
        act_copy.wait_send()
        skip_copy.wait_send()

    @pl.when(jnp.logical_not(first))
    def _():
        gact_copy.wait_send()
        gskip_copy.wait_send()


def network(fields, cotangent, depths, w_qkv, w_out, lat_total, lon_total):
    piece = 2 * D // (lat_total * lon_total)
    z_total = lat_total // 2
    vmem = pl.BlockSpec(memory_space=pltpu.VMEM)
    hbm = pl.BlockSpec(memory_space=pl.ANY)
    dma = pltpu.SemaphoreType.DMA
    scratch = [
        pltpu.VMEM((2, MAXL, D, 3 * D), BF16),
        pltpu.VMEM((2, MAXL, D, D), BF16),
        pltpu.VMEM((2, 8, 128), F32),
        pltpu.VMEM((2, HALF, D), BF16),
        pltpu.VMEM((2, 2, HALF, D), BF16),
        pltpu.VMEM((2, 2, HALF, D), BF16),
        pltpu.VMEM((TOK, D), F32),
        pltpu.VMEM((TOK, D), F32),
        pltpu.VMEM((2, 2, HALF, D), BF16),
        pltpu.VMEM((2, 2, HALF, D), BF16),
        pltpu.VMEM((2, 2, HALF, D), F32),
        pltpu.VMEM((2, 2, HALF, D), F32),
        pltpu.VMEM((2, 2, HALF, D), BF16),
        pltpu.VMEM((2, 2, HALF, D), BF16),
        pltpu.VMEM((2, 2, HALF, D), BF16),
        pltpu.VMEM((2, 2, HALF, 2 * D), BF16),
        pltpu.VMEM((2, 2, HALF, 2 * D), BF16),
        pltpu.VMEM((2, MAXL, TOK, D), F32),
        pltpu.VMEM((2, MAXL, TOK, 128), F32),
        pltpu.VMEM((2, MAXL, PAIRS, 2, TOK, TOK), F32),
        pltpu.VMEM((2, MAXL, PAIRS, 2 * TOK, 128), BF16),
        pltpu.VMEM((2, 3, TOK, 2 * D), BF16),
        pltpu.VMEM((4, 2, TOK, D), BF16),
        pltpu.VMEM((4, 2, TOK, D), BF16),
        pltpu.VMEM((4, 2, TOK, 2 * D), BF16),
        pltpu.VMEM((4, TOK, 2 * D), BF16),
        pltpu.VMEM((4, 2, 2, 2, 2, z_total, piece, D // 2), BF16),
        pltpu.VMEM((4, 2, 2, 2, z_total, piece, D // 2), BF16),
        pltpu.VMEM((4, 2, 2, 2, z_total, piece, D // 2), BF16),
        pltpu.VMEM((4, 2, 2, z_total, piece, D // 2), BF16),
        pltpu.VMEM((4, 2, 2, z_total, piece, D // 2), BF16),
        pltpu.VMEM((4, 2, z_total, piece, D // 2), BF16),
        pltpu.VMEM((4, z_total, 2, piece, D // 2), BF16),
        pltpu.VMEM((4, z_total - 1, 2, piece, D // 2), BF16),
        pltpu.VMEM((2, MAXL, 2, piece, D // 2), F32),
        pltpu.VMEM((MAXL, 2, piece, D // 2), F32),
        dma((MAXL, 2)),
        dma((MAXL, 2)),
        dma((MAXL, 2)),
        dma((2,)),
        dma((4,)),
        dma((2,)),
        dma((2,)),
        dma((2,)),
        dma((2,)),
        dma((2,)),
        dma((2,)),
        dma((2,)),
        dma((2,)),
        dma((2, 2)),
        dma((2, 2)),
        dma((2, 2)),
        dma((2, 2)),
        dma((4,)),
        dma((4,)),
        dma((4,)),
        dma((4,)),
        dma((4, 2, 3)),
        dma((4, 2, 3)),
        dma((4, z_total - 1)),
        dma((4, z_total - 1)),
        dma((MAXL,)),
        dma((MAXL,)),
    ]
    return pl.pallas_call(
        partial(body, lat_total, lon_total),
        out_shape=(
            jax.ShapeDtypeStruct(fields.shape, BF16),
            jax.ShapeDtypeStruct(fields.shape, F32),
            jax.ShapeDtypeStruct((MAXL, piece // 2, 3 * D), F32),
            jax.ShapeDtypeStruct((MAXL, piece // 2, D), F32),
        ),
        in_specs=[vmem, vmem, pl.BlockSpec(memory_space=pltpu.SMEM), hbm, hbm],
        out_specs=(vmem, vmem, vmem, vmem),
        scratch_shapes=scratch,
        compiler_params=pltpu.CompilerParams(
            collective_id=0, has_side_effects=True, vmem_limit_bytes=56 * 1024 * 1024
        ),
        name="network",
    )(fields, cotangent, depths, w_qkv, w_out)


def local(fields, cotangent, depths, w_qkv, w_out):
    out_rows, grad_rows, qkv_grad, out_grad = network(
        fields.transpose(1, 2, 0, 3), cotangent.transpose(1, 2, 0, 3), depths, w_qkv[0], w_out[0],
        lax.axis_size("lat"), lax.axis_size("lon"),
    )
    return (
        out_rows.transpose(2, 0, 1, 3)[None],
        grad_rows.transpose(2, 0, 1, 3)[None],
        qkv_grad[None],
        out_grad[None],
    )


def solution(mesh):
    placed = (
        P(None, "lat", "lon", None),
        P(None, "lat", "lon", None),
        P("segment"),
        P("segment", None, None, None),
        P("segment", None, None, None),
    )
    return jax.shard_map(
        local,
        mesh=mesh,
        in_specs=placed,
        out_specs=(
            P("segment", None, "lat", "lon", None),
            P("segment", None, "lat", "lon", None),
            P("segment", None, ("lat", "lon"), None),
            P("segment", None, ("lat", "lon"), None),
        ),
        check_vma=False,
    )
```

```python
from functools import partial

import jax
import jax.numpy as jnp
from jax import lax
from jax.experimental import pallas as pl
from jax.experimental.pallas import tpu as pltpu
from jax.sharding import PartitionSpec as P

HEADS = 8
HS = 64
WIN_LEV = 2
WIN_LON = 6
MAXL = 2
D = 512
PAIRS = 4
HALF = 72
TOK = 144
EPSILON = 1e-05
MESH = pl.DeviceIdType.MESH
F32 = jnp.float32
BF16 = jnp.bfloat16


def dot(a, b, contract):
    return lax.dot_general(a, b, ((contract[:1], contract[1:]), ((), ())), preferred_element_type=F32)


def normalize(stream):
    center = stream - jnp.mean(stream, axis=-1, keepdims=True)
    inverse = lax.rsqrt(jnp.mean(center * center, axis=-1, keepdims=True) + EPSILON)
    return (center * inverse, inverse)


def norm_back(scaled, inverse, gradient):
    middle = gradient - jnp.mean(gradient, axis=-1, keepdims=True)
    return inverse * (middle - scaled * jnp.mean(gradient * scaled, axis=-1, keepdims=True))


def split_heads(value):
    low = lax.broadcasted_iota(jnp.int32, value.shape, 1) < HS
    return jnp.concatenate([jnp.where(low, value, 0.0), jnp.where(low, 0.0, value)], axis=0).astype(BF16)


def join_heads(value):
    count = value.shape[0] // 2
    low = lax.broadcasted_iota(jnp.int32, (count, value.shape[1]), 1) < HS
    return jnp.where(low, value[:count], value[count:])


def window_forward(q2, k, v, valid):
    exponent = jnp.exp(dot(k, q2, (1, 1)) * (HS ** -0.5))
    if valid is not None:
        exponent = exponent * valid
    probs = exponent * (1.0 / jnp.sum(exponent, axis=0, keepdims=True))
    return probs, join_heads(dot(probs.astype(BF16), v, (0, 0)))


def window_backward(gm2, q2, k, v, probs):
    grad_probs = dot(v, gm2, (1, 1))
    inner = jnp.sum(probs * grad_probs, axis=0, keepdims=True)
    grad_scores = (probs * (grad_probs - inner) * (HS ** -0.5)).astype(BF16)
    gq = join_heads(dot(grad_scores, k, (0, 0)))
    gk = dot(grad_scores, q2, (1, 0))
    gv = dot(probs.astype(BF16), gm2, (1, 0))
    return gq, gk, gv


def picker(pair, shape, row_dim):
    rows = lax.broadcasted_iota(jnp.int32, shape, row_dim)
    cells = lax.broadcasted_iota(jnp.int32, shape, 1 - row_dim)
    return jnp.where(cells == 4 * (rows // 2) + 2 * pair + rows % 2, 1.0, 0.0)


def take_rows(ref, pair, half):
    cells = [ref[6 * half + row, col].astype(F32) for row in range(6) for col in range(WIN_LON)]
    cells = jnp.concatenate(cells, axis=0).astype(BF16)
    return dot(picker(pair, (HALF, TOK), 0).astype(BF16), cells, (1, 0)).astype(BF16)


def put_rows(ref, half, pairs):
    cells = 0.0
    for pair in range(2):
        cells = cells + lax.dot_general(
            picker(pair, (TOK, HALF), 1), pairs[pair], (((1,), (0,)), ((), ())),
            precision=lax.Precision.HIGHEST, preferred_element_type=F32,
        )
    for row in range(6):
        for col in range(WIN_LON):
            at = 4 * (WIN_LON * row + col)
            ref[6 * half + row, col] = cells[at : at + 4].astype(ref.dtype)


def body(
    lat_total, lon_total,
    fields_ref, cot_ref, depth_ref, wqkv_hbm, wout_hbm,
    out_ref, grad_ref, qkv_ref, wo_ref,
    wqkv_s, wout_s, act_s, stage, xin, gin, stream_s, g_s, outs, out_in, grads, grad_in, handoff,
    nrm, halo, rim, rim_in, xs, invs, probs_s, q2_s, kv_s, left, left_in, right, right_in,
    part_s, one_in, one_s, two_in, two_s, three_in, col_s, col_in, fin_s, fin_in,
    own_sem, w_send, w_recv, a_sem, i_sem, x_send, x_recv, g_send, g_recv, o_send, o_recv, s_send, s_recv,
    h_send, h_recv, r_send, r_recv, l_send, l_recv, t_send, t_recv,
    p_send, p_recv, z_send, z_recv, f_send, f_recv,
):
    seg = lax.axis_index("segment")
    lat = lax.axis_index("lat")
    lon = lax.axis_index("lon")
    core = lax.rem(seg, 2)
    first = seg < 2
    high = lax.rem(lat, 2)
    z_at = lat // 2
    z_total = lat_total // 2
    at_home = core == high
    has_far = jnp.where(core == 0, lat > 1, lat < lat_total - 2)
    other = seg + 1 - 2 * core
    partner = {"segment": other, "lat": lat, "lon": lon}
    across = {"segment": lax.rem(seg + 2, 4), "lat": lat, "lon": lon}
    beyond = {"segment": other, "lat": lax.rem(lat + lat_total - 2 + 4 * core, lat_total), "lon": lon}
    twin_lat = lat + 1 - 2 * high
    twin = {"segment": seg, "lat": twin_lat, "lon": lon}
    diagonal = {"segment": other, "lat": twin_lat, "lon": lon}

    def remote(src, dst, send, recv, to):
        return pltpu.make_async_remote_copy(
            src_ref=src, dst_ref=dst, send_sem=send, recv_sem=recv, device_id=to, device_id_type=MESH
        )

    barrier = pltpu.get_barrier_semaphore()
    pl.semaphore_signal(barrier, inc=1, device_id=partner, device_id_type=MESH)
    pl.semaphore_signal(barrier, inc=1, device_id=across, device_id_type=MESH)
    pl.semaphore_signal(barrier, inc=1, device_id=diagonal, device_id_type=MESH)

    @pl.when(has_far)
    def _():
        pl.semaphore_signal(barrier, inc=1, device_id=beyond, device_id_type=MESH)

    side, end = lax.rem((lon + 1) // 2, 2), lon // 2
    lon_side = lon + 1 - 2 * lax.rem(lon, 2)
    lon_end = lon_total - 1 - lon
    for peer_lon in (lon_side, lon_end):
        to = {"segment": seg, "lat": lat, "lon": peer_lon}
        pl.semaphore_signal(barrier, inc=1, device_id=to, device_id_type=MESH)
    pl.semaphore_signal(barrier, inc=1, device_id=twin, device_id_type=MESH)

    def z_peer(hop):
        return {"segment": seg, "lat": lax.rem(lat + 2 * hop, lat_total), "lon": lon}

    def greet_z(hop, carry):
        pl.semaphore_signal(barrier, inc=1, device_id=z_peer(hop), device_id_type=MESH)
        return carry

    lax.fori_loop(1, z_total, greet_z, 0)

    def own_w(layer):
        return (
            pltpu.make_async_copy(wqkv_hbm.at[layer], wqkv_s.at[core, layer], own_sem.at[layer, 0]),
            pltpu.make_async_copy(wout_hbm.at[layer], wout_s.at[core, layer], own_sem.at[layer, 1]),
        )

    def sent_w(layer):
        return (
            remote(wqkv_hbm.at[layer], wqkv_s.at[core, layer], w_send.at[layer, 0], w_recv.at[layer, 0], partner),
            remote(wout_hbm.at[layer], wout_s.at[core, layer], w_send.at[layer, 1], w_recv.at[layer, 1], partner),
        )

    def came_w(layer):
        other = 1 - core
        return (
            remote(wqkv_hbm.at[layer], wqkv_s.at[other, layer], w_send.at[layer, 0], w_recv.at[layer, 0], partner),
            remote(wout_hbm.at[layer], wout_s.at[other, layer], w_send.at[layer, 1], w_recv.at[layer, 1], partner),
        )

    for layer in range(MAXL):
        for copy in own_w(layer):
            copy.start()

    act_s[core] = jnp.broadcast_to((depth_ref[0] > 1).astype(F32), (8, 128))

    zeros = jnp.zeros((2, HALF, D), BF16)

    @pl.when(first)
    def _():
        xin[1] = zeros

        @pl.when(at_home)
        def _():
            xin[0, 0] = take_rows(fields_ref, high, 1 - core)
            xin[0, 1] = take_rows(fields_ref, high, core)
            stage[0] = take_rows(fields_ref, 1 - high, 1 - core)
            stage[1] = take_rows(fields_ref, 1 - high, core)

    @pl.when(jnp.logical_not(first))
    def _():
        gin[1] = zeros

        @pl.when(at_home)
        def _():
            gin[0, 0] = take_rows(cot_ref, high, 1 - core)
            gin[0, 1] = take_rows(cot_ref, high, core)
            stage[0] = take_rows(cot_ref, 1 - high, 1 - core)
            stage[1] = take_rows(cot_ref, 1 - high, core)

    @pl.when(jnp.logical_not(has_far))
    def _():
        for sl in range(2):
            halo[sl, 1] = jnp.zeros((HALF, D), BF16)
            rim_in[sl, 1] = jnp.zeros((HALF, 2 * D), BF16)

    pl.semaphore_wait(barrier, 6 + z_total - 1 + has_far.astype(jnp.int32))

    sent_act = remote(act_s.at[core], act_s.at[core], a_sem.at[0], a_sem.at[1], partner)
    came_act = remote(act_s.at[core], act_s.at[1 - core], a_sem.at[0], a_sem.at[1], partner)
    field_copy = remote(stage, xin.at[0], i_sem.at[0], i_sem.at[1], twin)
    target_copy = remote(stage, gin.at[0], i_sem.at[2], i_sem.at[3], twin)

    @pl.when(jnp.logical_and(at_home, first))
    def _():
        field_copy.start()

    @pl.when(jnp.logical_and(at_home, jnp.logical_not(first)))
    def _():
        target_copy.start()

    sent_act.start()
    for layer in range(MAXL):
        for copy in sent_w(layer):
            copy.start()

    def halo_near(sl):
        return remote(nrm.at[sl, 0], halo.at[sl, 0], h_send.at[sl, 0], h_recv.at[sl, 0], partner)

    def halo_far(sl):
        return remote(nrm.at[sl, 1], halo.at[sl, 1], h_send.at[sl, 1], h_recv.at[sl, 1], beyond)

    def rim_near(sl):
        return remote(rim.at[sl, 0], rim_in.at[sl, 0], r_send.at[sl, 0], r_recv.at[sl, 0], partner)

    def rim_far(sl):
        return remote(rim.at[sl, 1], rim_in.at[sl, 1], r_send.at[sl, 1], r_recv.at[sl, 1], beyond)

    def start_far(copy):
        @pl.when(has_far)
        def _():
            copy.start()

    def arrive_far(copy):
        @pl.when(has_far)
        def _():
            copy.wait_recv()

    def rows_left(unit):
        return remote(left.at[unit], left_in.at[unit], l_send.at[unit], l_recv.at[unit], partner)

    def rows_right(unit):
        return remote(right.at[unit, 1 - core], right_in.at[unit], t_send.at[unit], t_recv.at[unit], partner)

    def order_of(unit, tile):
        if tile == 0:
            return core == 1, core == 0
        return jnp.logical_and(core == 1, unit == 0), jnp.logical_and(core == 1, lax.rem(unit, 2) == 1)

    def arranged(unit, tile, of_side, of_end, of_twin):
        twin_first, side_first = order_of(unit, tile)
        if tile == 0:
            return jnp.where(twin_first, of_twin, of_side), of_end, jnp.where(twin_first, of_side, of_twin)
        one = jnp.where(twin_first, of_twin, jnp.where(side_first, of_side, of_end))
        return one, jnp.where(side_first, of_end, of_side), jnp.where(twin_first, of_end, of_twin)

    def pairs_of(unit, tile):
        ats = arranged(unit, tile, side, end, high)
        lats = arranged(unit, tile, lat, lat, twin_lat)
        lons = arranged(unit, tile, lon_side, lon_end, lon)
        return [(at, {"segment": seg, "lat": a, "lon": b}) for at, a, b in zip(ats, lats, lons)]

    def pair_copy(unit, tile, level):
        at, peer = pairs_of(unit, tile)[level]
        source = (part_s, one_s, two_s)[level].at[unit, tile, 1 - at]
        target = (one_in, two_in, three_in)[level].at[unit, tile]
        return remote(source, target, p_send.at[unit, tile, level], p_recv.at[unit, tile, level], peer)

    def pair_sum(unit, tile, level):
        at = pairs_of(unit, tile)[level][0]
        pair_copy(unit, tile, level).wait_recv()
        kept = (part_s, one_s, two_s)[level][unit, tile, at]
        return (kept.astype(F32) + (one_in, two_in, three_in)[level][unit, tile].astype(F32)).astype(BF16)

    def col_copy(unit, hop):
        return remote(
            col_s.at[unit, lax.rem(z_at + hop, z_total)], col_in.at[unit, hop - 1],
            z_send.at[unit, hop - 1], z_recv.at[unit, hop - 1], z_peer(hop),
        )

    def fin_copy(layer):
        return remote(fin_s.at[1 - core, layer], fin_in.at[layer], f_send.at[layer], f_recv.at[layer], partner)

    def weight_term(unit):
        rows_left(unit).wait_recv()
        rows_right(unit).wait_recv()
        normed = jnp.concatenate([left[unit, 0], left_in[unit, 0]], axis=0)
        second = jnp.concatenate([left[unit, core], left_in[unit, core]], axis=0)
        grads_low = jnp.concatenate([right[unit, core], right_in[unit]], axis=0)
        shape = (z_total, 2, lon_total, D // (lat_total * lon_total), D)
        for tile in range(2):
            term = dot(second if tile else normed, grads_low[:, D * tile : D * tile + D], (0, 0)).reshape(shape)
            term = jnp.concatenate([term[..., : D // 2], term[..., D // 2 :]], axis=3).astype(BF16)
            for x in range(2):
                for to in range(lon_total):
                    to_side, to_end = (to + 1) // 2 % 2, to // 2
                    one, two, three = arranged(unit, tile, to_side, to_end, x)
                    part_s[unit, tile, one, two, three] = term[:, x, to]

            @pl.when(first)
            def _():
                pair_copy(unit, tile, 0).start()

    def stage_two(unit):
        for tile in range(2):
            one_s[unit, tile] = pair_sum(unit, tile, 0)
            pair_copy(unit, tile, 1).start()

    def stage_three(unit):
        for tile in range(2):
            two_s[unit, tile] = pair_sum(unit, tile, 1)
            pair_copy(unit, tile, 2).start()

    def stage_four(unit):
        for tile in range(2):
            col_s[unit, :, tile] = pair_sum(unit, tile, 2)

        for hop in sorted(range(1, z_total), key=lambda hop: -min(hop, z_total - hop)):
            col_copy(unit, hop).start()

    def stage_five(unit):
        def add(hop, total):
            col_copy(unit, hop).wait_recv()
            return total + col_in[unit, hop - 1].astype(F32)

        owner, layer = unit // 2, unit % 2
        fin_s[owner, layer] = lax.fori_loop(1, z_total, add, col_s[unit, z_at].astype(F32))

        @pl.when(owner != core)
        def _():
            fin_copy(layer).start()

    act_copy = remote(outs.at[1], xin.at[0], x_send.at[0], x_recv.at[0], across)
    skip_copy = remote(outs.at[0], xin.at[1], x_send.at[1], x_recv.at[1], across)
    gact_copy = remote(handoff.at[0], gin.at[0], g_send.at[0], g_recv.at[0], across)
    gskip_copy = remote(handoff.at[1], gin.at[1], g_send.at[1], g_recv.at[1], across)

    def owner_of(sl):
        return {"segment": seg - core + sl, "lat": lat - high + core, "lon": lon}

    def out_copy(sl):
        return remote(outs.at[sl], out_in.at[high], o_send.at[sl], o_recv.at[high], owner_of(sl))

    def grad_copy(sl):
        return remote(grads.at[sl], grad_in.at[high], s_send.at[sl], s_recv.at[high], owner_of(sl))

    def hand_over(sl, copy, target, source):
        mine = jnp.logical_and(at_home, core == sl)

        @pl.when(mine)
        def _():
            target[high] = source[sl]

        @pl.when(jnp.logical_not(mine))
        def _():
            copy.start()

    key_at = lax.broadcasted_iota(jnp.int32, (TOK, 1), 0)
    valid_far = jnp.where(key_at < HALF, 1.0, has_far.astype(F32))

    def rows_of(ref, index):
        return jnp.concatenate([ref[index, 0].astype(F32), ref[index, 1].astype(F32)], axis=0)

    def weights_ready(sl, layer):
        @pl.when(core == sl)
        def _():
            for copy in own_w(layer):
                copy.wait()

        @pl.when(core != sl)
        def _():
            for copy in came_w(layer):
                copy.wait_recv()

    @pl.when(jnp.logical_not(first))
    def _():
        act_copy.wait_recv()

    @pl.when(jnp.logical_and(first, jnp.logical_not(at_home)))
    def _():
        field_copy.wait_recv()

    stream_s[...] = rows_of(xin, 0)

    def forward(sl, carry):
        stream = stream_s[...]
        scaled, inverse = normalize(stream)
        normed = scaled.astype(BF16)
        xs[sl, 0] = scaled
        invs[sl, 0] = jnp.broadcast_to(inverse, (TOK, 128))
        left[2 * sl, 0] = normed
        weights_ready(sl, 0)
        qkv = dot(normed, wqkv_s[sl, 0], (1, 0))
        kv_low = qkv[:, D:].astype(BF16)
        kv_s[sl, 0] = kv_low

        def attend(layer, part, qkv, keys, valid):
            mixed = []
            for p in range(PAIRS):
                at = slice(128 * p, 128 * p + 128)
                q2 = split_heads(qkv[HALF * part : HALF * part + HALF, at])
                q2_s[sl, layer, p, TOK * part : TOK * part + TOK] = q2
                probs, mix = window_forward(q2, keys[:, at], keys[:, D + 128 * p : D + 128 * p + 128], valid)
                probs_s[sl, layer, p, part] = probs
                mixed.append(mix)
            return jnp.concatenate(mixed, axis=1)

        mixed = [None, None]
        streams = [None, None]
        scales = [None, None]
        for part in (1, 0):
            rows = slice(HALF * part, HALF * part + HALF)
            mixed[part] = attend(0, part, qkv, kv_low, None)
            streams[part] = stream[rows] + dot(mixed[part].astype(BF16), wout_s[sl, 0], (1, 0))
            scaled, inverse = normalize(streams[part])
            nrm[sl, part] = scaled.astype(BF16)
            xs[sl, 1, rows] = scaled
            invs[sl, 1, rows] = jnp.broadcast_to(inverse, (HALF, 128))
            scales[part] = scaled
            if part == 1:
                start_far(halo_far(sl))
            else:
                halo_near(sl).start()
        left[2 * sl, 1] = jnp.concatenate(mixed, axis=0).astype(BF16)
        stream = jnp.concatenate(streams, axis=0)

        normed = jnp.concatenate(scales, axis=0).astype(BF16)
        left[2 * sl + 1, 0] = normed
        weights_ready(sl, 1)

        rows_left(2 * sl).start()
        qkv = dot(normed, wqkv_s[sl, 1], (1, 0))
        for part in (0, 1):
            if part == 0:
                halo_near(sl).wait_recv()
            else:
                arrive_far(halo_far(sl))
            beside = dot(halo[sl, part], wqkv_s[sl, 1, :, D:], (1, 0))
            keys = jnp.concatenate([qkv[HALF * part : HALF * part + HALF, D:], beside], axis=0).astype(BF16)
            kv_s[sl, 1 + part] = keys
            mixed[part] = attend(1, part, qkv, keys, valid_far if part == 1 else None)
        mixed_low = jnp.concatenate(mixed, axis=0).astype(BF16)
        left[2 * sl + 1, 1] = mixed_low

        rows_left(2 * sl + 1).start()

        @pl.when(core != sl)
        def _():
            came_act.wait_recv()

        stream = stream + act_s[sl][0:1, 0:1] * dot(mixed_low, wout_s[sl, 1], (1, 0))
        for part in range(2):
            outs[sl, part] = stream[HALF * part : HALF * part + HALF].astype(BF16)
        @pl.when(jnp.logical_and(first, sl == 1))
        def _():
            act_copy.start()

        hand_over(sl, out_copy(sl), out_in, outs)

        @pl.when(sl == 0)
        def _():
            @pl.when(first)
            def _():
                skip_copy.start()

            @pl.when(jnp.logical_not(first))
            def _():
                skip_copy.wait_recv()

            stream_s[...] = stream.astype(BF16).astype(F32) + rows_of(xin, 1)

        return carry

    lax.fori_loop(0, 2, forward, 0)

    @pl.when(first)
    def _():
        gact_copy.wait_recv()

    @pl.when(jnp.logical_not(jnp.logical_or(first, at_home)))
    def _():
        target_copy.wait_recv()

    g_s[...] = rows_of(gin, 0)

    def backward(step, carry):
        sl = 1 - step
        g = g_s[...]
        glow = (g * act_s[sl][0:1, 0:1]).astype(BF16)
        right[2 * sl + 1, 1, :, D:] = glow
        gm = dot(glow, wout_s[sl, 1], (1, 1))
        gq, pairs = [None, None], [None, None]
        for part in (1, 0):
            rows = slice(TOK * part, TOK * part + TOK)
            q, k, v = [], [], []
            for p in range(PAIRS):
                at = slice(128 * p, 128 * p + 128)
                vat = slice(D + 128 * p, D + 128 * p + 128)
                found = window_backward(
                    split_heads(gm[HALF * part : HALF * part + HALF, at]), q2_s[sl, 1, p, rows],
                    kv_s[sl, 1 + part, :, at], kv_s[sl, 1 + part, :, vat], probs_s[sl, 1, p, part],
                )
                q.append(found[0])
                k.append(found[1])
                v.append(found[2])
            gq[part] = jnp.concatenate(q, axis=1)
            pairs[part] = jnp.concatenate(k + v, axis=1)
            rim[sl, part] = pairs[part][HALF:].astype(BF16)
            if part == 1:
                start_far(rim_far(sl))
            else:
                rim_near(sl).start()
        query_low = jnp.concatenate(gq, axis=0).astype(BF16)
        right[2 * sl + 1, 0, :, :D] = query_low
        part = dot(query_low, wqkv_s[sl, 1, :, :D], (1, 1))

        @pl.when(step == 1)
        def _():
            weight_term(2)

            @pl.when(first)
            def _():
                stage_two(3)

        rim_near(sl).wait_recv()
        arrive_far(rim_far(sl))
        pairs_low = jnp.concatenate(
            [pairs[part][:HALF] + rim_in[sl, part].astype(F32) for part in range(2)], axis=0
        ).astype(BF16)
        right[2 * sl + 1, 0, :, D:] = pairs_low[:, :D]
        right[2 * sl + 1, 1, :, :D] = pairs_low[:, D:]

        rows_right(2 * sl + 1).start()
        part = part + dot(pairs_low, wqkv_s[sl, 1, :, D:], (1, 1))
        g = g + norm_back(xs[sl, 1], invs[sl, 1][:, 0:1], part)

        glow = g.astype(BF16)
        right[2 * sl, 1, :, D:] = glow
        gm = dot(glow, wout_s[sl, 0], (1, 1))
        gq, gk, gv = [], [], []
        for p in range(PAIRS):
            at = slice(128 * p, 128 * p + 128)
            vat = slice(D + 128 * p, D + 128 * p + 128)
            found = [
                window_backward(
                    split_heads(gm[HALF * part : HALF * part + HALF, at]), q2_s[sl, 0, p, TOK * part : TOK * part + TOK],
                    kv_s[sl, 0, :, at], kv_s[sl, 0, :, vat], probs_s[sl, 0, p, part],
                )
                for part in range(2)
            ]
            gq.append(jnp.concatenate([found[0][0], found[1][0]], axis=0))
            k = found[0][1] + found[1][1]
            v = found[0][2] + found[1][2]
            gk.append(k)
            gv.append(v)
        low = jnp.concatenate(gq + gk + gv, axis=1).astype(BF16)
        right[2 * sl, 0] = low[:, : 2 * D]
        right[2 * sl, 1, :, :D] = low[:, 2 * D :]

        rows_right(2 * sl).start()
        part = dot(low, wqkv_s[sl, 0], (1, 1))
        g = g + norm_back(xs[sl, 0], invs[sl, 0][:, 0:1], part)
        for part in range(2):
            grads[sl, part] = g[HALF * part : HALF * part + HALF]
        @pl.when(step == 0)
        def _():
            hand_over(sl, grad_copy(sl), grad_in, grads)

        @pl.when(jnp.logical_not(first))
        def _():
            for part in range(2):
                handoff[1 - step, part] = g[HALF * part : HALF * part + HALF].astype(BF16)

            @pl.when(step == 0)
            def _():
                gskip_copy.start()

            @pl.when(step == 1)
            def _():
                gact_copy.start()

        @pl.when(step == 0)
        def _():
            @pl.when(first)
            def _():
                gskip_copy.wait_recv()

            g_s[...] = g + rows_of(gin, 1)

        @pl.when(jnp.logical_or(first, step == 1))
        def _():
            weight_term(2 * sl + 1)

        return carry

    lax.fori_loop(0, 2, backward, 0)
    weight_term(0)

    @pl.when(jnp.logical_not(first))
    def _():
        weight_term(3)
        for unit in (3, 2, 1, 0):
            for tile in range(2):
                pair_copy(unit, tile, 0).start()
        stage_two(3)

    hand_over(0, grad_copy(0), grad_in, grads)
    stage_two(2)
    stage_three(3)
    stage_two(1)
    stage_three(2)
    stage_two(0)
    stage_four(3)
    stage_three(1)
    stage_four(2)
    stage_three(0)
    stage_four(1)
    stage_five(3)
    for pair in range(2):
        came = jnp.logical_not(jnp.logical_and(at_home, high == pair))

        @pl.when(came)
        def _():
            remote(outs.at[0], out_in.at[pair], o_send.at[0], o_recv.at[pair], partner).wait_recv()
            remote(grads.at[0], grad_in.at[pair], s_send.at[0], s_recv.at[pair], partner).wait_recv()

    for half in range(2):
        index = (1 - high) if half == 0 else high
        put_rows(out_ref, half, [out_in[pair, index].astype(F32) for pair in range(2)])
        put_rows(grad_ref, half, [grad_in[pair, index] for pair in range(2)])

    stage_five(2)
    stage_four(0)
    stage_five(1)
    stage_five(0)

    piece = D // (lat_total * lon_total)
    for layer in range(MAXL):
        fin_copy(layer).wait_recv()
        mine, came = fin_s[core, layer], fin_in[layer]
        first_half = jnp.where(core == 0, mine, came)
        second_half = jnp.where(core == 0, came, mine)
        for side_at in range(2):
            at = D // 2 * side_at
            rows = slice(piece * side_at, piece * side_at + piece)
            qkv_ref[layer, :, at : at + D // 2] = first_half[0, rows]
            qkv_ref[layer, :, D + at : D + at + D // 2] = first_half[1, rows]
            qkv_ref[layer, :, 2 * D + at : 2 * D + at + D // 2] = second_half[0, rows]
            wo_ref[layer, :, at : at + D // 2] = second_half[1, rows]

    sent_act.wait_send()

    for layer in range(MAXL):
        for copy in sent_w(layer):
            copy.wait_send()
        fin_copy(layer).wait_send()
    for unit in range(4):
        rows_left(unit).wait_send()
        rows_right(unit).wait_send()

        for tile in range(2):
            for level in range(3):
                pair_copy(unit, tile, level).wait_send()

        def sent(hop, carry):
            col_copy(unit, hop).wait_send()
            return carry

        lax.fori_loop(1, z_total, sent, 0)
    for sl in range(2):
        @pl.when(jnp.logical_not(jnp.logical_and(at_home, core == sl)))
        def _():
            out_copy(sl).wait_send()
            grad_copy(sl).wait_send()

        halo_near(sl).wait_send()
        rim_near(sl).wait_send()

        @pl.when(has_far)
        def _():
            halo_far(sl).wait_send()
            rim_far(sl).wait_send()

    @pl.when(jnp.logical_and(at_home, first))
    def _():
        field_copy.wait_send()

    @pl.when(jnp.logical_and(at_home, jnp.logical_not(first)))
    def _():
        target_copy.wait_send()

    @pl.when(first)
    def _():
        act_copy.wait_send()
        skip_copy.wait_send()

    @pl.when(jnp.logical_not(first))
    def _():
        gact_copy.wait_send()
        gskip_copy.wait_send()


def network(fields, cotangent, depths, w_qkv, w_out, lat_total, lon_total):
    piece = 2 * D // (lat_total * lon_total)
    z_total = lat_total // 2
    vmem = pl.BlockSpec(memory_space=pltpu.VMEM)
    hbm = pl.BlockSpec(memory_space=pl.ANY)
    dma = pltpu.SemaphoreType.DMA
    scratch = [
        pltpu.VMEM((2, MAXL, D, 3 * D), BF16),
        pltpu.VMEM((2, MAXL, D, D), BF16),
        pltpu.VMEM((2, 8, 128), F32),
        pltpu.VMEM((2, HALF, D), BF16),
        pltpu.VMEM((2, 2, HALF, D), BF16),
        pltpu.VMEM((2, 2, HALF, D), BF16),
        pltpu.VMEM((TOK, D), F32),
        pltpu.VMEM((TOK, D), F32),
        pltpu.VMEM((2, 2, HALF, D), BF16),
        pltpu.VMEM((2, 2, HALF, D), BF16),
        pltpu.VMEM((2, 2, HALF, D), F32),
        pltpu.VMEM((2, 2, HALF, D), F32),
        pltpu.VMEM((2, 2, HALF, D), BF16),
        pltpu.VMEM((2, 2, HALF, D), BF16),
        pltpu.VMEM((2, 2, HALF, D), BF16),
        pltpu.VMEM((2, 2, HALF, 2 * D), BF16),
        pltpu.VMEM((2, 2, HALF, 2 * D), BF16),
        pltpu.VMEM((2, MAXL, TOK, D), F32),
        pltpu.VMEM((2, MAXL, TOK, 128), F32),
        pltpu.VMEM((2, MAXL, PAIRS, 2, TOK, TOK), F32),
        pltpu.VMEM((2, MAXL, PAIRS, 2 * TOK, 128), BF16),
        pltpu.VMEM((2, 3, TOK, 2 * D), BF16),
        pltpu.VMEM((4, 2, TOK, D), BF16),
        pltpu.VMEM((4, 2, TOK, D), BF16),
        pltpu.VMEM((4, 2, TOK, 2 * D), BF16),
        pltpu.VMEM((4, TOK, 2 * D), BF16),
        pltpu.VMEM((4, 2, 2, 2, 2, z_total, piece, D // 2), BF16),
        pltpu.VMEM((4, 2, 2, 2, z_total, piece, D // 2), BF16),
        pltpu.VMEM((4, 2, 2, 2, z_total, piece, D // 2), BF16),
        pltpu.VMEM((4, 2, 2, z_total, piece, D // 2), BF16),
        pltpu.VMEM((4, 2, 2, z_total, piece, D // 2), BF16),
        pltpu.VMEM((4, 2, z_total, piece, D // 2), BF16),
        pltpu.VMEM((4, z_total, 2, piece, D // 2), BF16),
        pltpu.VMEM((4, z_total - 1, 2, piece, D // 2), BF16),
        pltpu.VMEM((2, MAXL, 2, piece, D // 2), F32),
        pltpu.VMEM((MAXL, 2, piece, D // 2), F32),
        dma((MAXL, 2)),
        dma((MAXL, 2)),
        dma((MAXL, 2)),
        dma((2,)),
        dma((4,)),
        dma((2,)),
        dma((2,)),
        dma((2,)),
        dma((2,)),
        dma((2,)),
        dma((2,)),
        dma((2,)),
        dma((2,)),
        dma((2, 2)),
        dma((2, 2)),
        dma((2, 2)),
        dma((2, 2)),
        dma((4,)),
        dma((4,)),
        dma((4,)),
        dma((4,)),
        dma((4, 2, 3)),
        dma((4, 2, 3)),
        dma((4, z_total - 1)),
        dma((4, z_total - 1)),
        dma((MAXL,)),
        dma((MAXL,)),
    ]
    return pl.pallas_call(
        partial(body, lat_total, lon_total),
        out_shape=(
            jax.ShapeDtypeStruct(fields.shape, BF16),
            jax.ShapeDtypeStruct(fields.shape, F32),
            jax.ShapeDtypeStruct((MAXL, piece // 2, 3 * D), F32),
            jax.ShapeDtypeStruct((MAXL, piece // 2, D), F32),
        ),
        in_specs=[vmem, vmem, pl.BlockSpec(memory_space=pltpu.SMEM), hbm, hbm],
        out_specs=(vmem, vmem, vmem, vmem),
        scratch_shapes=scratch,
        compiler_params=pltpu.CompilerParams(
            collective_id=0, has_side_effects=True, vmem_limit_bytes=56 * 1024 * 1024
        ),
        name="network",
    )(fields, cotangent, depths, w_qkv, w_out)


def copier(*refs):
    count = len(refs) // 2
    for source, target in zip(refs[:count], refs[count:]):
        target[...] = source[...]


def copied(*arrays):
    vmem = pl.BlockSpec(memory_space=pltpu.VMEM)
    return pl.pallas_call(
        copier,
        out_shape=tuple(jax.ShapeDtypeStruct(a.shape, a.dtype) for a in arrays),
        in_specs=[vmem] * len(arrays),
        out_specs=(vmem,) * len(arrays),
        name="copied",
    )(*arrays)


def local(fields, cotangent, depths, w_qkv, w_out):
    out_rows, grad_rows, qkv_grad, out_grad = network(
        fields.transpose(1, 2, 0, 3), cotangent.transpose(1, 2, 0, 3), depths, w_qkv[0], w_out[0],
        lax.axis_size("lat"), lax.axis_size("lon"),
    )
    out_rows, grad_rows, qkv_grad, out_grad = copied(out_rows, grad_rows, qkv_grad, out_grad)
    return (
        out_rows.transpose(2, 0, 1, 3)[None],
        grad_rows.transpose(2, 0, 1, 3)[None],
        qkv_grad[None],
        out_grad[None],
    )


def solution(mesh):
    placed = (
        P(None, "lat", "lon", None),
        P(None, "lat", "lon", None),
        P("segment"),
        P("segment", None, None, None),
        P("segment", None, None, None),
    )
    return jax.shard_map(
        local,
        mesh=mesh,
        in_specs=placed,
        out_specs=(
            P("segment", None, "lat", "lon", None),
            P("segment", None, "lat", "lon", None),
            P("segment", None, ("lat", "lon"), None),
            P("segment", None, ("lat", "lon"), None),
        ),
        check_vma=False,
    )
```
